128 devices in a mesh: member: 8 (over y, x_hi), space: 8 (over z, x_lo), step: 2 (over core).
Axes of the slice: x: 4 (x_hi: 2, x_lo: 2; x = x_hi * 2 + x_lo), y: 4, z: 4, core: 2. Of those that a mesh axis runs over, the one named last changes fastest.
Arguments:
- state: bfloat16 [16, 2048, 1024], P('member', 'space'), may hold values from -6 to 6
- norm_gain: float32 [1024], replicated, may hold values from 0.5 to 1.5
- w_query: bfloat16 [1024, 1024], replicated, may hold values from -2 to 2
- w_key: bfloat16 [1024, 1024], replicated, may hold values from -2 to 2
- w_value: bfloat16 [1024, 1024], replicated, may hold values from -0.1875 to 0.1875
- w_out: bfloat16 [1024, 1024], replicated, may hold values from -0.1875 to 0.1875
- w_decode: bfloat16 [1024, 128], replicated, may hold values from -0.1875 to 0.1875
- neighbours: int32 [16, 4], P('space'), may hold values from 0 to 15, as said below
- counts: int32 [16], P('space'), may hold values from 2 to 4
- group_ids: int32 [128], replicated, may hold values from 0 to 7, as said below
- area: float32 [2048], P('space'), may hold values from 0.3 to 9
- truth: bfloat16 [2, 2048, 128], P('step', 'space'), may hold values from -6 to 6
Outputs:
- new_state: bfloat16 [2, 16, 2048, 1024], P('step', 'member', 'space')
- losses: float32 [2, 8], P('step')
The draws below stay inside these ranges and needn't reach their ends.
Inputs may be any that keep to these rules, and one draw needn't show every extreme that they name: neighbours[b, 0] = b; every other entry lies within 2 blocks of b, and entries reach that distance. `group_ids`: each group holds exactly 16 variables.
All inputs are finite; a program needn't handle non-finite values.
Results may differ from the reference program's by a relative error of at most 0.0065.
Values may be sent and summed in bfloat16 or wider, within the bound.
A program may use at most 128 MiB of HBM per device.

```python
import math
import jax
import jax.numpy as jnp
from jax import lax

D = 1024
HEADS = 16
HEAD = 64
VARS = 128
GROUPS = 8
BLOCK = 128
NB = 4
MEMBERS = 16
POINTS = 2048
NBLK = 16
BLK_DEV = 2
STEPS = 2


def projection_draw(key, own_key):
    own = jax.random.normal(own_key, (D, D), jnp.float32)
    weight = own / math.sqrt(D)
    return jnp.clip(weight, -2.0, 2.0).astype(jnp.bfloat16)


def draw_w_query(key, part):
    return projection_draw(key, jax.random.fold_in(key, 11))


def draw_w_key(key, part):
    return projection_draw(key, jax.random.fold_in(key, 12))


def draw_neighbours(key, part):
    key = jax.random.fold_in(key, 21)
    blocks = jnp.arange(NBLK, dtype=jnp.int32)[:, None]
    offsets = jax.random.randint(key, (NBLK, NB), -BLK_DEV, BLK_DEV + 1, dtype=jnp.int32)
    offsets = offsets.at[0, 1].set(BLK_DEV)
    chosen = jnp.clip(blocks + offsets, 0, NBLK - 1)
    slots = jnp.arange(NB, dtype=jnp.int32)[None, :]
    return jnp.where(slots == 0, blocks, chosen).astype(jnp.int32)


def draw_counts(key, part):
    key = jax.random.fold_in(key, 22)
    drawn = jax.random.randint(key, (NBLK,), 2, NB + 1, dtype=jnp.int32)
    return drawn.at[0].set(NB)


def draw_group_ids(key, part):
    key = jax.random.fold_in(key, 23)
    order = jax.random.permutation(key, VARS)
    return (order % GROUPS).astype(jnp.int32)


def draw_area(key, part):
    key = jax.random.fold_in(key, 24)
    ramp = 1.0 + 2.0 * jnp.arange(POINTS, dtype=jnp.float32) / (POINTS - 1)
    factor = jnp.exp(jax.random.uniform(key, (POINTS,), jnp.float32, math.log(0.5), math.log(2.0)))
    return (ramp * factor).astype(jnp.float32)


def level_of(key, extent, split, least, high):
    def one(axis_at, parts):
        draws = jax.random.uniform(jax.random.fold_in(jax.random.fold_in(key, 6), axis_at), (parts,), jnp.float32, least / len(split), high / len(split))
        return jnp.repeat(jnp.exp(draws), extent[axis_at] // parts).reshape((-1,) + (1,) * (len(extent) - axis_at - 1))

    loudness = one(*split[0])
    for cut in split[1:]:
        loudness = loudness * one(*cut)
    return loudness


def normal_values(key, extent, scale, most, shards=(), kind=jnp.bfloat16):
    entries = jax.random.normal(key, extent, jnp.float32) * scale
    if len(shards) > 0:
        entries = level_of(key, extent, shards, -0.22, 0.18) * entries
    return jnp.clip(entries, min=-most, max=most).astype(kind)


def setup_inputs(seed: int = 0) -> dict:
    key_list = jax.random.split(jax.random.key(seed), 13)
    return {
        "state": normal_values(key_list[0], (MEMBERS, POINTS, D), 1.0, 6.0, ((0, 8), (1, 8))),
        "norm_gain": jnp.clip(1.0 + 0.1 * jax.random.normal(key_list[1], (D,), jnp.float32), 0.5, 1.5),
        "w_query": draw_w_query(jax.random.fold_in(key_list[12], 71), 0),
        "w_key": draw_w_key(jax.random.fold_in(key_list[12], 71), 0),
        "w_value": normal_values(key_list[4], (D, D), D ** -0.5, 0.1875),
        "w_out": normal_values(key_list[5], (D, D), D ** -0.5, 0.1875),
        "w_decode": normal_values(key_list[6], (D, VARS), D ** -0.5, 0.1875),
        "neighbours": draw_neighbours(jax.random.fold_in(key_list[12], 71), 0),
        "counts": draw_counts(jax.random.fold_in(key_list[12], 71), 0),
        "group_ids": draw_group_ids(jax.random.fold_in(key_list[12], 71), 0),
        "area": draw_area(jax.random.fold_in(key_list[12], 71), 0),
        "truth": normal_values(key_list[11], (STEPS, POINTS, VARS), 1.0, 6.0, ((0, 2), (1, 8))),
    }


alpha_fair = 0.95

def rms_normed(fields, gain):
    values = fields.astype(jnp.float32)
    factor = lax.rsqrt(lax.optimization_barrier(jnp.mean(values * values, axis=-1, keepdims=True)) + 1e-06)
    return (values * factor * gain).astype(jnp.bfloat16)

def project(rows, weight):
    return jnp.dot(rows, weight, preferred_element_type=jnp.float32).astype(jnp.bfloat16)

def layer_member(fields, norm_gain, w_query, w_key, w_value, w_out, neighbours, counts):
    normed = rms_normed(fields, norm_gain)
    queries = project(normed, w_query).reshape(NBLK, BLOCK, HEADS, HEAD).astype(jnp.float32)
    keys = project(normed, w_key).reshape(NBLK, BLOCK, HEADS, HEAD)
    values = project(normed, w_value).reshape(NBLK, BLOCK, HEADS, HEAD)
    near_keys = keys[neighbours].reshape(NBLK, NB * BLOCK, HEADS, HEAD).astype(jnp.float32)
    near_values = values[neighbours].reshape(NBLK, NB * BLOCK, HEADS, HEAD).astype(jnp.float32)
    valid = jnp.repeat(jnp.arange(NB)[None, :] < counts[:, None], BLOCK, axis=1)
    scores = jnp.einsum('bqhe,bkhe->bhqk', queries, near_keys) / math.sqrt(HEAD)
    scores = jnp.where(valid[:, None, None, :], scores, -1e+30)
    highest = lax.optimization_barrier(jnp.max(scores, axis=-1, keepdims=True))
    raised = jnp.exp(scores - highest)
    probs = (raised / lax.optimization_barrier(jnp.sum(raised, axis=-1, keepdims=True))).astype(jnp.bfloat16)
    attended = jnp.einsum('bhqk,bkhe->bqhe', probs.astype(jnp.float32), near_values)
    attended = attended.astype(jnp.bfloat16).reshape(POINTS, D)
    update = jnp.dot(attended, w_out, preferred_element_type=jnp.float32)
    return (fields.astype(jnp.float32) + update).astype(jnp.bfloat16)

def crps_terms(preds, target):
    values = preds.astype(jnp.float32)
    goal = target.astype(jnp.float32)
    members = values.shape[0]
    skill = lax.optimization_barrier(jnp.mean(jnp.abs(values - goal[None]), axis=0))
    spread = lax.optimization_barrier(jnp.sum(lax.map(lambda single: lax.optimization_barrier(jnp.sum(jnp.abs(values - single[None]), axis=0)), values), axis=0))
    epsilon = (1.0 - alpha_fair) / members
    return skill - (1.0 - epsilon) * spread / (2.0 * members * (members - 1))

def group_loss(terms, area, group_ids):
    onehot = (group_ids[:, None] == jnp.arange(GROUPS)[None, :]).astype(jnp.float32)
    weighted = jnp.dot(area, terms, precision=lax.Precision.HIGHEST)
    totals = jnp.dot(weighted, onehot, precision=lax.Precision.HIGHEST)
    return totals / (jnp.sum(area) * (VARS // GROUPS))

def reference(state, norm_gain, w_query, w_key, w_value, w_out, w_decode, neighbours, counts, group_ids, area, truth):
    current = state
    states = []
    losses = []
    for step_number in range(STEPS):
        current = lax.map(lambda member: layer_member(member, norm_gain, w_query, w_key, w_value, w_out, neighbours, counts), current)
        preds = jnp.dot(current.reshape(MEMBERS * POINTS, D), w_decode, preferred_element_type=jnp.float32)
        preds = preds.astype(jnp.bfloat16).reshape(MEMBERS, POINTS, VARS)
        losses.append(group_loss(crps_terms(preds, truth[step_number]), area, group_ids))
        states.append(current)
    return (jnp.stack(states), jnp.stack(losses))
```

```python
import functools

import jax
import jax.numpy as jnp
from jax import lax
from jax.experimental import pallas as pl
from jax.experimental.pallas import tpu as pltpu
from jax.sharding import PartitionSpec as P

D = 1024
HEAD = 64
VARS = 128
GROUPS = 8
BLOCK = 128
ROWS = 256
MEMBERS = 16
SLOTS = 4
STEPS = 2
ALPHA = 0.95
CHUNKS = 4
CHUNK = ROWS // CHUNKS
TILE = 256
SHARE = 32
MESH = pl.DeviceIdType.MESH
BF = jnp.bfloat16
F32 = jnp.float32


def dot(a, b):
    return jnp.dot(a, b, preferred_element_type=F32)


def dot_t(a, b):
    return lax.dot_general(a, b, (((1,), (1,)), ((), ())), preferred_element_type=F32)


def kernel(
    state, gain, w_query, w_key, w_value, w_out, w_decode, neighbours, counts, group_ids, area, truth,
    out, loss,
    cur, halo, nrm, wbuf, wdec, qkv0, qkv1, att, preds, gathered, goal, gains, groups, areas, meta_v, used_v, meta_s,
    red1, red2,
    lsem, xs, xr, zs, zr, ks, kr, osend, orecv, ps, pr, ms, mr, r1s, r1r, r2s, r2r,
):
    m, s, c = (lax.axis_index(name) for name in ("member", "space", "step"))
    z, xl = lax.div(s, 2), lax.rem(s, 2)
    local = xl == c
    foreign = xl != c
    partner = {"space": 2 * z + 1 - xl}
    other = {"step": 1 - c}
    has_z = jnp.where(c == 1, z < 3, z > 0)
    z_target = {"space": s + 4 * c - 2, "step": 1 - c}
    qkvs = (qkv0, qkv1)

    def fetch(i, src, dst):
        return pltpu.make_async_copy(src, dst, lsem.at[i])

    loads = [
        fetch(0, w_key, wbuf.at[1]),
        fetch(1, w_value, wbuf.at[2]),
        fetch(2, w_query, wbuf.at[0]),
        fetch(3, w_out, wbuf.at[3]),
        fetch(4, w_decode, wdec),
        fetch(5, gain, gains),
        fetch(6, group_ids, groups),
        fetch(7, area, areas),
        fetch(8, truth.at[0, pl.ds(pl.multiple_of(m * SHARE, SHARE), SHARE)], goal),
    ]

    def own_chunk(i):
        part = pl.ds(i * CHUNK, CHUNK)
        return pltpu.make_async_copy(state.at[xl, part], cur.at[0, part], xr.at[i])

    def x_chunk(i):
        part = pl.ds(i * CHUNK, CHUNK)
        return pltpu.make_async_remote_copy(
            state.at[1 - xl, part], cur.at[0, part], xs.at[i], xr.at[i], device_id=partner, device_id_type=MESH
        )

    def z_part(t, i, size):
        part = pl.ds(i * size, size)
        return pltpu.make_async_remote_copy(
            cur.at[t, part], halo.at[t, part], zs.at[t, i], zr.at[t, i], device_id=z_target, device_id_type=MESH
        )

    def meta_copy():
        return pltpu.make_async_remote_copy(
            meta_v.at[0], meta_v.at[1], ms.at[0], mr.at[0], device_id=partner, device_id_type=MESH
        )

    def kv_copy(t, j):
        return pltpu.make_async_remote_copy(
            qkvs[t].at[j, pl.ds(2, 2)],
            qkvs[t].at[j, pl.ds(4 * c, 2)],
            ks.at[t, j - 1], kr.at[t, j - 1], device_id=other, device_id_type=MESH,
        )

    def out_remote(t, b, slot):
        part = pl.ds(b * BLOCK, BLOCK)
        return pltpu.make_async_remote_copy(
            cur.at[t + 1, part], out.at[0, slot, part], osend.at[t, b], orecv.at[slot, b],
            device_id={"space": 2 * z + c, "step": t}, device_id_type=MESH,
        )

    def out_local(t, b, slot):
        part = pl.ds(b * BLOCK, BLOCK)
        return pltpu.make_async_copy(cur.at[t + 1, part], out.at[0, slot, part], orecv.at[slot, b])

    def preds_copy(t, i):
        return pltpu.make_async_remote_copy(
            preds.at[t, pl.ds(i * SHARE, SHARE)], gathered.at[2 * m + xl], ps.at[t, i], pr.at[0],
            device_id={"member": i, "space": 2 * z + c, "step": t}, device_id_type=MESH,
        )

    def preds_own(t, i):
        return pltpu.make_async_copy(preds.at[t, pl.ds(i * SHARE, SHARE)], gathered.at[2 * m + xl], pr.at[0])

    barrier = pltpu.get_barrier_semaphore()

    def greet(**device):
        pl.semaphore_signal(barrier, inc=1, device_id=device, device_id_type=MESH)

    for copy in loads[:1]:
        copy.start()

    def greet_plane(i, _):
        mate = lax.rem(m + lax.div(i, 4), 8)
        x_mate = lax.rem(xl + lax.rem(lax.div(i, 2), 2), 2)
        core = lax.rem(c + lax.rem(i, 2), 2)
        greet(member=mate, space=2 * z + x_mate, step=core)
        return 0

    lax.fori_loop(1, 32, greet_plane, 0)
    for dz in range(1, 4):
        for x_mate in range(2):
            greet(space=2 * lax.rem(z + dz, 4) + x_mate)

    @pl.when(has_z)
    def _():
        greet(**z_target)

    @pl.when(local)
    def _():
        for i in range(CHUNKS):
            own_chunk(i).start()

    for copy in loads[1:]:
        copy.start()

    column = lax.broadcasted_iota(jnp.int32, (8, 128), 1)
    row8 = lax.broadcasted_iota(jnp.int32, (8, 128), 0)
    meta = jnp.zeros((8, 128), jnp.int32)
    for b in range(2):
        for slot in range(SLOTS):
            meta = jnp.where(column == b * SLOTS + slot, neighbours[b, slot], meta)
    meta = jnp.where(row8 == 2, counts[0], jnp.where(row8 == 3, counts[1], meta))
    meta_v[0] = meta

    @pl.when(jnp.logical_not(has_z))
    def _():
        halo[...] = jnp.zeros_like(halo)

    pl.semaphore_wait(barrier, 37 + has_z.astype(jnp.int32))

    @pl.when(local)
    def _():
        for i in range(CHUNKS):
            x_chunk(i).start()
        meta_copy().start()
        to_scalars = pltpu.make_async_copy(meta_v.at[0], meta_s, lsem.at[9])
        to_scalars.start()
        to_scalars.wait()
        used_v[...] = meta_v[0, 2:4, :]

    for i in range(CHUNKS):
        own_chunk(i).wait()

        @pl.when(has_z)
        def _():
            z_part(0, i, CHUNK).start()

    @pl.when(foreign)
    def _():
        meta_copy().wait_recv()
        to_scalars = pltpu.make_async_copy(meta_v.at[1], meta_s, lsem.at[9])
        to_scalars.start()
        to_scalars.wait()
        used_v[...] = meta_v[1, 2:4, :]

    loads[5].wait()

    def normalise(src, row, rows, dst):
        def step(i, _):
            part = pl.ds(pl.multiple_of(row + i * 32, 32), 32)
            values = src[part, :].astype(F32)
            factor = lax.rsqrt(jnp.mean(values * values, axis=-1, keepdims=True) + 1e-06)
            dst[part, :] = (values * factor * gains[...]).astype(BF)
            return 0

        lax.fori_loop(0, rows // 32, step, 0)

    def project(row, rows, w, dst, dst_block):
        def step(n, _):
            cols = pl.ds(pl.multiple_of(n * TILE, TILE), TILE)
            values = dot(nrm[pl.ds(row, rows), :], wbuf[w, :, cols]).astype(BF)
            for i in range(rows // BLOCK):
                dst[w, dst_block + i, :, cols] = values[i * BLOCK : (i + 1) * BLOCK]
            return 0

        lax.fori_loop(0, D // TILE, step, 0)

    first_block = 4 * z + 2 * c - 2
    head_of = lax.broadcasted_iota(jnp.int32, (1, TILE), 1)
    masks = [
        jnp.where((head_of >= HEAD * i) & (head_of < HEAD * (i + 1)), 0.125, 0.0).astype(BF) for i in range(4)
    ]
    lane = lax.broadcasted_iota(jnp.int32, (BLOCK, TILE), 1)

    def attend(qkv, b):
        near = [jnp.clip(meta_s[0, b * SLOTS + slot] - first_block, 0, 5) for slot in range(SLOTS)]
        used = used_v[b : b + 1, :]
        bias = [jnp.where(used > slot, 0.0, -1e30) for slot in range(SLOTS)]

        def step(g, _):
            cols = pl.ds(pl.multiple_of(g * TILE, TILE), TILE)
            query = qkv[0, 2 + b, :, cols]
            query = jnp.concatenate([query * mask for mask in masks], axis=0)
            keys = [jnp.concatenate([qkv[1, near[i + k], :, cols] for k in range(2)], axis=0) for i in (0, 2)]
            values = jnp.concatenate([qkv[2, near[i], :, cols] for i in range(SLOTS)], axis=0)
            first = dot_t(query, keys[0])
            second = dot_t(query, keys[1])
            second = jnp.concatenate([second[:, :BLOCK] + bias[2], second[:, BLOCK:] + bias[3]], axis=1)
            scores = jnp.concatenate([first, second], axis=1)
            highest = jnp.max(scores, axis=-1, keepdims=True)
            raised = jnp.exp(scores - highest)
            total = jnp.sum(raised, axis=-1, keepdims=True)
            mixed = dot(raised.astype(BF), values) * (1.0 / total)
            parts = [mixed[i * BLOCK : (i + 1) * BLOCK] for i in range(4)]
            attended = parts[3]
            for i in (2, 1, 0):
                attended = jnp.where(lane < HEAD * (i + 1), parts[i], attended)
            att[:, cols] = attended.astype(BF)
            return 0

        lax.fori_loop(0, D // TILE, step, 0)

    def update(t, b):
        part = pl.ds(b * BLOCK, BLOCK)

        def step(n, _):
            cols = pl.ds(pl.multiple_of(n * TILE, TILE), TILE)
            values = cur[t, part, cols].astype(F32) + dot(att[...], wbuf[3, :, cols])
            cur[t + 1, part, cols] = values.astype(BF)
            return 0

        lax.fori_loop(0, D // TILE, step, 0)

    for t in range(STEPS):
        qkv = qkvs[t]
        out_here = local & (c == t)
        normalise(cur.at[t], 0, ROWS, nrm)
        for j in (1, 2, 0):
            if t == 0:
                loads[(2, 0, 1)[j]].wait()
            project(0, ROWS, j, qkv, 2)
            if j:
                kv_copy(t, j).start()
        size = CHUNK if t == 0 else BLOCK
        for b in range(2):

            @pl.when(has_z)
            def _():
                for i in range(BLOCK // size):
                    z_part(t, b * (BLOCK // size) + i, size).wait_recv()

            normalise(halo.at[t], b * BLOCK, BLOCK, nrm)
            for j in (1, 2):
                project(b * BLOCK, BLOCK, j, qkv, 4 * c + b)
        for j in (1, 2):
            kv_copy(t, j).wait_recv()
        if t == 0:
            loads[3].wait()
        for b in range(2):
            attend(qkv, b)
            update(t, b)
            if t + 1 < STEPS:

                @pl.when(has_z)
                def _():
                    z_part(t + 1, b, BLOCK).start()

            @pl.when(out_here)
            def _():
                out_local(t, b, xl).start()

            @pl.when(jnp.logical_not(out_here))
            def _():
                out_remote(t, b, xl).start()

        if t == 0:
            loads[4].wait()
        preds[t] = dot(cur[t + 1], wdec[...]).astype(BF)
        for i in range(8):
            own = out_here & (m == i)

            @pl.when(own)
            def _():
                preds_own(t, i).start()

            @pl.when(jnp.logical_not(own))
            def _():
                preds_copy(t, i).start()

    for copy in loads[6:9]:
        copy.wait()
    pltpu.make_async_copy(gathered, gathered, pr.at[0]).wait()
    epsilon = (1.0 - ALPHA) / MEMBERS
    weighted = jnp.zeros((1, VARS), F32)
    mine = lax.broadcasted_iota(jnp.int32, (SHARE, ROWS), 0) + m * SHARE
    spread_out = jnp.where(lax.broadcasted_iota(jnp.int32, (SHARE, ROWS), 1) == mine, areas[...], 0.0)
    weights = jnp.sum(spread_out, axis=1, keepdims=True)
    for i in range(SHARE // 16):
        part = slice(i * 16, i * 16 + 16)
        values = [gathered[k, part, :].astype(F32) for k in range(MEMBERS)]
        wanted = goal[part, :].astype(F32)
        skill = jnp.zeros((16, VARS), F32)
        spread = jnp.zeros((16, VARS), F32)
        for k in range(MEMBERS):
            skill += jnp.abs(values[k] - wanted)
            for j in range(k):
                spread += jnp.abs(values[k] - values[j])
        terms = skill * (1.0 / MEMBERS) - spread * ((1.0 - epsilon) / (MEMBERS * (MEMBERS - 1)))
        weighted += jnp.sum(terms * weights[part], axis=0, keepdims=True)
    row = lax.broadcasted_iota(jnp.int32, (8, VARS), 0)
    tile = jnp.where(row == 0, weighted, jnp.where(row == 1, jnp.sum(weights, axis=0, keepdims=True), 0.0))

    def exchange(tile, buffer, send, recv, me, axis):
        buffer[me] = tile

        def copy(i):
            return pltpu.make_async_remote_copy(
                buffer.at[me], buffer.at[me], send.at[i - 1], recv.at[0],
                device_id={axis: lax.rem(me + i, 8)}, device_id_type=MESH,
            )

        for i in range(1, 8):
            copy(i).start()
        rest = buffer.at[pl.ds(0, 7)]
        pltpu.make_async_copy(rest, rest, recv.at[0]).wait()
        total = buffer[0]
        for i in range(1, 8):
            total += buffer[i]
        return total, copy

    tile, copy1 = exchange(tile, red1, r1s, r1r, m, "member")
    tile, copy2 = exchange(tile, red2, r2s, r2r, s, "space")
    slot = lax.broadcasted_iota(jnp.int32, (1, GROUPS), 1)
    result = jnp.zeros((1, GROUPS), F32)
    for g in range(GROUPS):
        share = jnp.sum(jnp.where(groups[...] == g, tile[0:1], 0.0), axis=1, keepdims=True)
        result = jnp.where(slot == g, share, result)
    loss[...] = result / (tile[1:2, :GROUPS] * (VARS // GROUPS))

    for slot_xl in range(2):
        for b in range(2):
            out_local(0, b, slot_xl).wait()

    @pl.when(local)
    def _():
        for i in range(CHUNKS):
            x_chunk(i).wait_send()
        meta_copy().wait_send()

    @pl.when(has_z)
    def _():
        for i in range(CHUNKS):
            z_part(0, i, CHUNK).wait_send()
        for i in range(2):
            z_part(1, i, BLOCK).wait_send()

    for t in range(STEPS):
        out_here = local & (c == t)
        for j in (1, 2):
            kv_copy(t, j).wait_send()

        @pl.when(jnp.logical_not(out_here))
        def _():
            for b in range(2):
                out_remote(t, b, xl).wait_send()

        for i in range(8):

            @pl.when(jnp.logical_not(out_here & (m == i)))
            def _():
                preds_copy(t, i).wait_send()

    for i in range(1, 8):
        copy1(i).wait_send()
        copy2(i).wait_send()


def shards(
    state, norm_gain, w_query, w_key, w_value, w_out, w_decode, neighbours, counts, group_ids, area, truth
):
    anywhere = pl.BlockSpec(memory_space=pl.ANY)
    scalars = pl.BlockSpec(memory_space=pltpu.SMEM)
    dma = pltpu.SemaphoreType.DMA
    return pl.pallas_call(
        kernel,
        out_shape=(
            jax.ShapeDtypeStruct((1, 2, ROWS, D), BF),
            jax.ShapeDtypeStruct((1, GROUPS), F32),
        ),
        in_specs=[anywhere] * 7 + [scalars] * 2 + [anywhere] * 3,
        out_specs=(anywhere, pl.BlockSpec(memory_space=pltpu.VMEM)),
        scratch_shapes=[
            pltpu.VMEM((STEPS + 1, ROWS, D), BF),
            pltpu.VMEM((STEPS, ROWS, D), BF),
            pltpu.VMEM((ROWS, D), BF),
            pltpu.VMEM((4, D, D), BF),
            pltpu.VMEM((D, VARS), BF),
            pltpu.VMEM((3, 6, BLOCK, D), BF),
            pltpu.VMEM((3, 6, BLOCK, D), BF),
            pltpu.VMEM((BLOCK, D), BF),
            pltpu.VMEM((STEPS, ROWS, VARS), BF),
            pltpu.VMEM((MEMBERS, SHARE, VARS), BF),
            pltpu.VMEM((SHARE, VARS), BF),
            pltpu.VMEM((1, D), F32),
            pltpu.VMEM((1, VARS), jnp.int32),
            pltpu.VMEM((1, ROWS), F32),
            pltpu.VMEM((2, 8, 128), jnp.int32),
            pltpu.VMEM((2, 128), jnp.int32),
            pltpu.SMEM((8, 128), jnp.int32),
            pltpu.VMEM((8, 8, VARS), F32),
            pltpu.VMEM((8, 8, VARS), F32),
            dma((10,)),
            dma((CHUNKS,)),
            dma((CHUNKS,)),
            dma((STEPS, CHUNKS)),
            dma((STEPS, CHUNKS)),
            dma((STEPS, 2)),
            dma((STEPS, 2)),
            dma((STEPS, 2)),
            dma((2, 2)),
            dma((STEPS, 8)),
            dma((1,)),
            dma((1,)),
            dma((1,)),
            dma((7,)),
            dma((1,)),
            dma((7,)),
            dma((1,)),
        ],
        compiler_params=pltpu.CompilerParams(
            collective_id=0, has_side_effects=True, vmem_limit_bytes=60 * 1024 * 1024
        ),
        name="rollout",
    )(
        state, norm_gain.reshape(1, D), w_query, w_key, w_value, w_out, w_decode, neighbours, counts,
        group_ids.reshape(1, VARS), area.reshape(1, ROWS), truth,
    )


def solution(mesh):
    return jax.shard_map(
        shards,
        mesh=mesh,
        in_specs=(
            P("member", "space", None),
            P(),
            P(),
            P(),
            P(),
            P(),
            P(),
            P("space", None),
            P("space"),
            P(),
            P("space"),
            P("step", "space", None),
        ),
        out_specs=(P("step", "member", "space", None), P("step", None)),
        check_vma=False,
    )
```

```python
import functools

import jax
import jax.numpy as jnp
from jax import lax
from jax.experimental import pallas as pl
from jax.experimental.pallas import tpu as pltpu
from jax.sharding import PartitionSpec as P

D = 1024
HEAD = 64
VARS = 128
GROUPS = 8
BLOCK = 128
ROWS = 256
MEMBERS = 16
SLOTS = 4
STEPS = 2
ALPHA = 0.95
CHUNKS = 8
CHUNK = ROWS // CHUNKS
TILE = 256
SHARE = 32
MESH = pl.DeviceIdType.MESH
BF = jnp.bfloat16
F32 = jnp.float32


def dot(a, b):
    return jnp.dot(a, b, preferred_element_type=F32)


def dot_t(a, b):
    return lax.dot_general(a, b, (((1,), (1,)), ((), ())), preferred_element_type=F32)


def kernel(
    state, gain, w_query, w_key, w_value, w_out, w_decode, neighbours, counts, group_ids, area, truth,
    out, loss,
    cur, halo, nrm, wbuf, wdec, qkv0, qkv1, att, preds, gathered, goal, gains, groups, areas, meta_v, used_v, meta_s,
    red1, red2,
    lsem, xs, xr, zs, zr, ks, kr, osend, orecv, ps, pr, ms, mr, r1s, r1r, r2s, r2r,
):
    m, s, c = (lax.axis_index(name) for name in ("member", "space", "step"))
    z, xl = lax.div(s, 2), lax.rem(s, 2)
    local = xl == c
    foreign = xl != c
    partner = {"space": 2 * z + 1 - xl}
    other = {"step": 1 - c}
    has_z = jnp.where(c == 1, z < 3, z > 0)
    z_target = {"space": s + 4 * c - 2, "step": 1 - c}
    qkvs = (qkv0, qkv1)

    def fetch(i, src, dst):
        return pltpu.make_async_copy(src, dst, lsem.at[i])

    loads = [
        fetch(0, w_key, wbuf.at[1]),
        fetch(1, w_value, wbuf.at[2]),
        fetch(2, w_query, wbuf.at[0]),
        fetch(3, w_out, wbuf.at[3]),
        fetch(4, w_decode, wdec),
        fetch(5, gain, gains),
        fetch(6, group_ids, groups),
        fetch(7, area, areas),
        fetch(8, truth.at[0, pl.ds(pl.multiple_of(m * SHARE, SHARE), SHARE)], goal),
    ]

    def own_chunk(i):
        part = pl.ds(pl.multiple_of(i * CHUNK, CHUNK), CHUNK)
        return pltpu.make_async_copy(state.at[xl, part], cur.at[0, part], xr.at[i])

    def x_chunk(i):
        part = pl.ds(pl.multiple_of(i * CHUNK, CHUNK), CHUNK)
        return pltpu.make_async_remote_copy(
            state.at[1 - xl, part], cur.at[0, part], xs.at[i], xr.at[i],
            device_id={"space": 2 * z + 1 - xl, "step": xl}, device_id_type=MESH,
        )

    def z_part(t, i, size):
        part = pl.ds(pl.multiple_of(i * size, size), size)
        return pltpu.make_async_remote_copy(
            cur.at[t, part], halo.at[t, part], zs.at[t, i], zr.at[t, i], device_id=z_target, device_id_type=MESH
        )

    def meta_copy():
        return pltpu.make_async_remote_copy(
            meta_v.at[0], meta_v.at[1], ms.at[0], mr.at[0], device_id=partner, device_id_type=MESH
        )

    def kv_copy(t, j, b):
        return pltpu.make_async_remote_copy(
            qkvs[t].at[j, 2 + b], qkvs[t].at[j, 4 * c + b], ks.at[t, j - 1, b], kr.at[t, j - 1, b],
            device_id=other, device_id_type=MESH,
        )

    def out_remote(t, b, slot):
        part = pl.ds(pl.multiple_of(b * BLOCK, BLOCK), BLOCK)
        return pltpu.make_async_remote_copy(
            cur.at[t + 1, part], out.at[0, slot, part], osend.at[t, b], orecv.at[slot, b],
            device_id={"space": 2 * z + c, "step": t}, device_id_type=MESH,
        )

    def out_local(t, b, slot):
        part = pl.ds(pl.multiple_of(b * BLOCK, BLOCK), BLOCK)
        return pltpu.make_async_copy(cur.at[t + 1, part], out.at[0, slot, part], orecv.at[slot, b])

    def preds_copy(t, i):
        return pltpu.make_async_remote_copy(
            preds.at[t, pl.ds(i * SHARE, SHARE)], gathered.at[2 * m + xl], ps.at[t, i], pr.at[0],
            device_id={"member": i, "space": 2 * z + c, "step": t}, device_id_type=MESH,
        )

    def preds_own(t, i):
        return pltpu.make_async_copy(preds.at[t, pl.ds(i * SHARE, SHARE)], gathered.at[2 * m + xl], pr.at[0])

    barrier = pltpu.get_barrier_semaphore()

    def greet(**device):
        pl.semaphore_signal(barrier, inc=1, device_id=device, device_id_type=MESH)

    for copy in loads[:1]:
        copy.start()

    def greet_plane(i, _):
        mate = lax.rem(m + lax.div(i, 4), 8)
        x_mate = lax.rem(xl + lax.rem(lax.div(i, 2), 2), 2)
        core = lax.rem(c + lax.rem(i, 2), 2)
        greet(member=mate, space=2 * z + x_mate, step=core)
        return 0

    lax.fori_loop(1, 32, greet_plane, 0)
    for dz in range(1, 4):
        for x_mate in range(2):
            greet(space=2 * lax.rem(z + dz, 4) + x_mate)

    @pl.when(has_z)
    def _():
        greet(**z_target)

    @pl.when(local)
    def _():
        for i in range(CHUNKS):
            own_chunk(i).start()

    for copy in loads[1:]:
        copy.start()

    column = lax.broadcasted_iota(jnp.int32, (8, 128), 1)
    row8 = lax.broadcasted_iota(jnp.int32, (8, 128), 0)
    meta = jnp.zeros((8, 128), jnp.int32)
    for b in range(2):
        for slot in range(SLOTS):
            meta = jnp.where(column == b * SLOTS + slot, neighbours[b, slot], meta)
    meta = jnp.where(row8 == 2, counts[0], jnp.where(row8 == 3, counts[1], meta))
    meta_v[0] = meta

    @pl.when(jnp.logical_not(has_z))
    def _():
        halo[...] = jnp.zeros_like(halo)

    pl.semaphore_wait(barrier, 37 + has_z.astype(jnp.int32))

    for i in range(CHUNKS // 2):
        x_chunk(2 * i + foreign.astype(jnp.int32)).start()

    @pl.when(local)
    def _():
        meta_copy().start()
        to_scalars = pltpu.make_async_copy(meta_v.at[0], meta_s, lsem.at[9])
        to_scalars.start()
        to_scalars.wait()
        used_v[...] = meta_v[0, 2:4, :]

    def forward(i):
        own_chunk(i).wait()

        @pl.when(has_z)
        def _():
            z_part(0, i, CHUNK).start()

    def normalise(src, row, rows, dst):
        def step(i, _):
            part = pl.ds(pl.multiple_of(row + i * 64, 64), 64)
            values = src[part, :].astype(F32)
            factor = lax.rsqrt(jnp.mean(values * values, axis=-1, keepdims=True) + 1e-06)
            dst[part, :] = (values * factor * gains[...]).astype(BF)
            return 0

        lax.fori_loop(0, rows // 64, step, 0)

    def project(row, rows, w, dst, dst_block):
        values = dot(nrm[pl.ds(row, rows), :], wbuf[w]).astype(BF)
        for i in range(rows // BLOCK):
            dst[w, dst_block + i] = values[i * BLOCK : (i + 1) * BLOCK]

    first_block = 4 * z + 2 * c - 2
    head_of = lax.broadcasted_iota(jnp.int32, (1, TILE), 1)
    masks = [
        jnp.where((head_of >= HEAD * i) & (head_of < HEAD * (i + 1)), 0.125, 0.0).astype(BF) for i in range(4)
    ]
    lane = lax.broadcasted_iota(jnp.int32, (BLOCK, TILE), 1)

    def attend(qkv, b):
        near = [jnp.clip(meta_s[0, b * SLOTS + slot] - first_block, 0, 5) for slot in range(SLOTS)]
        used = used_v[pl.ds(b, 1), :]
        bias = [jnp.where(used > slot, 0.0, -1e30) for slot in range(SLOTS)]

        def scores(g):
            cols = slice(g * TILE, (g + 1) * TILE)
            query = qkv[0, 2 + b, :, cols]
            query = jnp.concatenate([query * mask for mask in masks], axis=0)
            keys = [jnp.concatenate([qkv[1, near[i + k], :, cols] for k in range(2)], axis=0) for i in (0, 2)]
            first = dot_t(query, keys[0])
            second = dot_t(query, keys[1])
            second = jnp.concatenate([second[:, :BLOCK] + bias[2], second[:, BLOCK:] + bias[3]], axis=1)
            return jnp.concatenate([first, second], axis=1)

        ready = scores(0)
        for g in range(D // TILE):
            later = scores(g + 1) if g + 1 < D // TILE else None
            cols = slice(g * TILE, (g + 1) * TILE)
            values = jnp.concatenate([qkv[2, near[i], :, cols] for i in range(SLOTS)], axis=0)
            highest = jnp.max(ready, axis=-1, keepdims=True)
            raised = jnp.exp(ready - highest)
            total = jnp.sum(raised, axis=-1, keepdims=True)
            mixed = dot(raised.astype(BF), values) * (1.0 / total)
            parts = [mixed[i * BLOCK : (i + 1) * BLOCK] for i in range(4)]
            attended = parts[3]
            for i in (2, 1, 0):
                attended = jnp.where(lane < HEAD * (i + 1), parts[i], attended)
            att[:, cols] = attended.astype(BF)
            ready = later

    def update(t, b):
        part = pl.ds(pl.multiple_of(b * BLOCK, BLOCK), BLOCK)
        cur[t + 1, part, :] = (cur[t, part, :].astype(F32) + dot(att[...], wbuf[3])).astype(BF)

    def decode(t):
        preds[t] = dot(cur[t + 1], wdec[...]).astype(BF)
        for i in range(8):
            own = local & (c == t) & (m == i)

            @pl.when(own)
            def _():
                preds_own(t, i).start()

            @pl.when(jnp.logical_not(own))
            def _():
                preds_copy(t, i).start()

    for t in range(STEPS):
        qkv = qkvs[t]
        out_here = local & (c == t)
        if t == 0:
            for i in range(4):
                forward(i)
            loads[5].wait()
            normalise(cur.at[0], 0, BLOCK, nrm)
            forward(4)
            for j, load, chunk in ((1, 0, 5), (2, 1, 6), (0, 2, 7)):
                loads[load].wait()
                project(0, BLOCK, j, qkv, 2)
                if j:
                    kv_copy(0, j, 0).start()
                forward(chunk)
            normalise(cur.at[0], BLOCK, BLOCK, nrm)
            for j in (1, 2, 0):
                project(BLOCK, BLOCK, j, qkv, 3)
                if j:
                    kv_copy(0, j, 1).start()

            @pl.when(foreign)
            def _():
                meta_copy().wait_recv()
                to_scalars = pltpu.make_async_copy(meta_v.at[1], meta_s, lsem.at[9])
                to_scalars.start()
                to_scalars.wait()
                used_v[...] = meta_v[1, 2:4, :]

        else:
            normalise(cur.at[t], 0, ROWS, nrm)
            for j in (1, 2, 0):
                project(0, ROWS, j, qkv, 2)
                if j:
                    for b in range(2):
                        kv_copy(t, j, b).start()
            loads[4].wait()
            decode(t - 1)

        size = CHUNK if t == 0 else BLOCK
        for b in range(2):

            @pl.when(has_z)
            def _():
                for i in range(BLOCK // size):
                    z_part(t, b * (BLOCK // size) + i, size).wait_recv()

            normalise(halo.at[t], b * BLOCK, BLOCK, nrm)
            for j in (1, 2):
                project(b * BLOCK, BLOCK, j, qkv, 4 * c + b)
        for j in (1, 2):
            for b in range(2):
                kv_copy(t, j, b).wait_recv()
        if t == 0:
            loads[3].wait()

        def block(b, _):
            attend(qkv, b)
            update(t, b)
            if t + 1 < STEPS:

                @pl.when(has_z)
                def _():
                    z_part(t + 1, b, BLOCK).start()

            @pl.when(out_here)
            def _():
                out_local(t, b, xl).start()

            @pl.when(jnp.logical_not(out_here))
            def _():
                out_remote(t, b, xl).start()

            return 0

        lax.fori_loop(0, 2, block, 0)
    decode(STEPS - 1)

    for copy in loads[6:9]:
        copy.wait()
    pltpu.make_async_copy(gathered, gathered, pr.at[0]).wait()
    epsilon = (1.0 - ALPHA) / MEMBERS
    weighted = jnp.zeros((1, VARS), F32)
    mine = lax.broadcasted_iota(jnp.int32, (SHARE, ROWS), 0) + m * SHARE
    spread_out = jnp.where(lax.broadcasted_iota(jnp.int32, (SHARE, ROWS), 1) == mine, areas[...], 0.0)
    weights = jnp.sum(spread_out, axis=1, keepdims=True)
    for i in range(SHARE // 16):
        part = slice(i * 16, i * 16 + 16)
        values = [gathered[k, part, :].astype(F32) for k in range(MEMBERS)]
        wanted = goal[part, :].astype(F32)
        skill = jnp.zeros((16, VARS), F32)
        spread = jnp.zeros((16, VARS), F32)
        for k in range(MEMBERS):
            skill += jnp.abs(values[k] - wanted)
            for j in range(k):
                spread += jnp.abs(values[k] - values[j])
        terms = skill * (1.0 / MEMBERS) - spread * ((1.0 - epsilon) / (MEMBERS * (MEMBERS - 1)))
        weighted += jnp.sum(terms * weights[part], axis=0, keepdims=True)
    row = lax.broadcasted_iota(jnp.int32, (8, VARS), 0)
    tile = jnp.where(row == 0, weighted, jnp.where(row == 1, jnp.sum(weights, axis=0, keepdims=True), 0.0))

    def exchange(tile, buffer, send, recv, me, axis):
        buffer[me] = tile

        def copy(i):
            return pltpu.make_async_remote_copy(
                buffer.at[me], buffer.at[me], send.at[i - 1], recv.at[0],
                device_id={axis: lax.rem(me + i, 8)}, device_id_type=MESH,
            )

        for i in range(1, 8):
            copy(i).start()
        rest = buffer.at[pl.ds(0, 7)]
        pltpu.make_async_copy(rest, rest, recv.at[0]).wait()
        total = buffer[0]
        for i in range(1, 8):
            total += buffer[i]
        return total, copy

    tile, copy1 = exchange(tile, red1, r1s, r1r, m, "member")
    tile, copy2 = exchange(tile, red2, r2s, r2r, s, "space")
    slot = lax.broadcasted_iota(jnp.int32, (1, GROUPS), 1)
    result = jnp.zeros((1, GROUPS), F32)
    for g in range(GROUPS):
        share = jnp.sum(jnp.where(groups[...] == g, tile[0:1], 0.0), axis=1, keepdims=True)
        result = jnp.where(slot == g, share, result)
    loss[...] = result / (tile[1:2, :GROUPS] * (VARS // GROUPS))

    for slot_xl in range(2):
        for b in range(2):
            out_local(0, b, slot_xl).wait()

    for i in range(CHUNKS // 2):
        x_chunk(2 * i + foreign.astype(jnp.int32)).wait_send()

    @pl.when(local)
    def _():
        meta_copy().wait_send()

    @pl.when(has_z)
    def _():
        for i in range(CHUNKS):
            z_part(0, i, CHUNK).wait_send()
        for i in range(2):
            z_part(1, i, BLOCK).wait_send()

    for t in range(STEPS):
        out_here = local & (c == t)
        for j in (1, 2):
            for b in range(2):
                kv_copy(t, j, b).wait_send()

        @pl.when(jnp.logical_not(out_here))
        def _():
            for b in range(2):
                out_remote(t, b, xl).wait_send()

        for i in range(8):

            @pl.when(jnp.logical_not(out_here & (m == i)))
            def _():
                preds_copy(t, i).wait_send()

    for i in range(1, 8):
        copy1(i).wait_send()
        copy2(i).wait_send()


def shards(
    state, norm_gain, w_query, w_key, w_value, w_out, w_decode, neighbours, counts, group_ids, area, truth
):
    anywhere = pl.BlockSpec(memory_space=pl.ANY)
    scalars = pl.BlockSpec(memory_space=pltpu.SMEM)
    dma = pltpu.SemaphoreType.DMA
    return pl.pallas_call(
        kernel,
        out_shape=(
            pltpu.VMEM((1, 2, ROWS, D), BF),
            jax.ShapeDtypeStruct((1, GROUPS), F32),
        ),
        in_specs=[anywhere] * 7 + [scalars] * 2 + [anywhere] * 3,
        out_specs=(anywhere, pl.BlockSpec(memory_space=pltpu.VMEM)),
        scratch_shapes=[
            pltpu.VMEM((STEPS + 1, ROWS, D), BF),
            pltpu.VMEM((STEPS, ROWS, D), BF),
            pltpu.VMEM((ROWS, D), BF),
            pltpu.VMEM((4, D, D), BF),
            pltpu.VMEM((D, VARS), BF),
            pltpu.VMEM((3, 6, BLOCK, D), BF),
            pltpu.VMEM((3, 6, BLOCK, D), BF),
            pltpu.VMEM((BLOCK, D), BF),
            pltpu.VMEM((STEPS, ROWS, VARS), BF),
            pltpu.VMEM((MEMBERS, SHARE, VARS), BF),
            pltpu.VMEM((SHARE, VARS), BF),
            pltpu.VMEM((1, D), F32),
            pltpu.VMEM((1, VARS), jnp.int32),
            pltpu.VMEM((1, ROWS), F32),
            pltpu.VMEM((2, 8, 128), jnp.int32),
            pltpu.VMEM((2, 128), jnp.int32),
            pltpu.SMEM((8, 128), jnp.int32),
            pltpu.VMEM((8, 8, VARS), F32),
            pltpu.VMEM((8, 8, VARS), F32),
            dma((10,)),
            dma((CHUNKS,)),
            dma((CHUNKS,)),
            dma((STEPS, CHUNKS)),
            dma((STEPS, CHUNKS)),
            dma((STEPS, 2, 2)),
            dma((STEPS, 2, 2)),
            dma((STEPS, 2)),
            dma((2, 2)),
            dma((STEPS, 8)),
            dma((1,)),
            dma((1,)),
            dma((1,)),
            dma((7,)),
            dma((1,)),
            dma((7,)),
            dma((1,)),
        ],
        compiler_params=pltpu.CompilerParams(
            collective_id=0, has_side_effects=True, vmem_limit_bytes=60 * 1024 * 1024
        ),
        name="rollout",
    )(
        state, norm_gain.reshape(1, D), w_query, w_key, w_value, w_out, w_decode, neighbours, counts,
        group_ids.reshape(1, VARS), area.reshape(1, ROWS), truth,
    )


def solution(mesh):
    return jax.shard_map(
        shards,
        mesh=mesh,
        in_specs=(
            P("member", "space", None),
            P(),
            P(),
            P(),
            P(),
            P(),
            P(),
            P("space", None),
            P("space"),
            P(),
            P("space"),
            P("step", "space", None),
        ),
        out_specs=(P("step", "member", "space", None), P("step", None)),
        check_vma=False,
    )
```

```python
import functools

import jax
import jax.numpy as jnp
from jax import lax
from jax.experimental import pallas as pl
from jax.experimental.pallas import tpu as pltpu
from jax.sharding import PartitionSpec as P

D = 1024
HEAD = 64
VARS = 128
GROUPS = 8
BLOCK = 128
ROWS = 256
MEMBERS = 16
SLOTS = 4
STEPS = 2
ALPHA = 0.95
CHUNKS = 8
CHUNK = ROWS // CHUNKS
TILE = 256
SHARE = 16
MESH = pl.DeviceIdType.MESH
BF = jnp.bfloat16
F32 = jnp.float32


def dot(a, b):
    return jnp.dot(a, b, preferred_element_type=F32)


def dot_t(a, b):
    return lax.dot_general(a, b, (((1,), (1,)), ((), ())), preferred_element_type=F32)


def kernel(
    state, gain, w_query, w_key, w_value, w_out, w_decode, neighbours, counts, group_ids, area, truth,
    out, loss,
    cur, halo, nrm, wbuf, wdec, qkv0, qkv1, att, preds, gathered, goal, gains, groups, areas, meta_v, used_v, meta_s,
    red1, red2,
    lsem, xs, xr, zs, zr, ks, kr, osend, orecv, ps, pr, ms, mr, r1s, r1r, r2s, r2r,
):
    m, s, c = (lax.axis_index(name) for name in ("member", "space", "step"))
    z, xl = lax.div(s, 2), lax.rem(s, 2)
    local = xl == c
    foreign = xl != c
    partner = {"space": 2 * z + 1 - xl}
    other = {"step": 1 - c}
    has_z = jnp.where(c == 1, z < 3, z > 0)
    z_target = {"space": s + 4 * c - 2, "step": 1 - c}
    qkvs = (qkv0, qkv1)

    def fetch(i, src, dst):
        return pltpu.make_async_copy(src, dst, lsem.at[i])

    loads = [
        fetch(0, w_key, wbuf.at[1]),
        fetch(1, w_value, wbuf.at[2]),
        fetch(2, w_query, wbuf.at[0]),
        fetch(3, w_out, wbuf.at[3]),
        fetch(4, w_decode, wdec),
        fetch(5, gain, gains),
        fetch(6, group_ids, groups),
        fetch(7, area, areas),
        fetch(8, truth.at[0, pl.ds(pl.multiple_of(m * SHARE, SHARE), SHARE)], goal.at[0]),
        fetch(9, truth.at[0, pl.ds(pl.multiple_of(BLOCK + m * SHARE, SHARE), SHARE)], goal.at[1]),
    ]

    def own_chunk(i):
        part = pl.ds(pl.multiple_of(i * CHUNK, CHUNK), CHUNK)
        return pltpu.make_async_copy(state.at[xl, part], cur.at[0, part], xr.at[i])

    def x_chunk(i):
        part = pl.ds(pl.multiple_of(i * CHUNK, CHUNK), CHUNK)
        return pltpu.make_async_remote_copy(
            state.at[1 - xl, part], cur.at[0, part], xs.at[i], xr.at[i],
            device_id={"space": 2 * z + 1 - xl, "step": xl}, device_id_type=MESH,
        )

    def z_part(t, i, size):
        part = pl.ds(pl.multiple_of(i * size, size), size)
        return pltpu.make_async_remote_copy(
            cur.at[t, part], halo.at[t, part], zs.at[t, i], zr.at[t, i], device_id=z_target, device_id_type=MESH
        )

    def meta_copy():
        return pltpu.make_async_remote_copy(
            meta_v.at[0], meta_v.at[1], ms.at[0], mr.at[0], device_id=partner, device_id_type=MESH
        )

    def kv_copy(t, j, b):
        return pltpu.make_async_remote_copy(
            qkvs[t].at[j, 2 + b], qkvs[t].at[j, 4 * c + b], ks.at[t, j - 1, b], kr.at[t, j - 1, b],
            device_id=other, device_id_type=MESH,
        )

    def out_remote(t, b, slot):
        part = pl.ds(pl.multiple_of(b * BLOCK, BLOCK), BLOCK)
        return pltpu.make_async_remote_copy(
            cur.at[t + 1, part], out.at[0, slot, part], osend.at[t, b], orecv.at[slot, b],
            device_id={"space": 2 * z + c, "step": t}, device_id_type=MESH,
        )

    def out_local(t, b, slot):
        part = pl.ds(pl.multiple_of(b * BLOCK, BLOCK), BLOCK)
        return pltpu.make_async_copy(cur.at[t + 1, part], out.at[0, slot, part], orecv.at[slot, b])

    def preds_copy(t, b, i):
        return pltpu.make_async_remote_copy(
            preds.at[t, b, pl.ds(i * SHARE, SHARE)], gathered.at[b, 2 * m + xl], ps.at[t, b, i], pr.at[0],
            device_id={"member": i, "space": 2 * z + c, "step": t}, device_id_type=MESH,
        )

    def preds_own(t, b, i):
        return pltpu.make_async_copy(
            preds.at[t, b, pl.ds(i * SHARE, SHARE)], gathered.at[b, 2 * m + xl], pr.at[0]
        )

    barrier = pltpu.get_barrier_semaphore()

    def greet(**device):
        pl.semaphore_signal(barrier, inc=1, device_id=device, device_id_type=MESH)

    for copy in loads[:1]:
        copy.start()

    def greet_plane(i, _):
        mate = lax.rem(m + lax.div(i, 4), 8)
        x_mate = lax.rem(xl + lax.rem(lax.div(i, 2), 2), 2)
        core = lax.rem(c + lax.rem(i, 2), 2)
        greet(member=mate, space=2 * z + x_mate, step=core)
        return 0

    lax.fori_loop(1, 32, greet_plane, 0)
    for dz in range(1, 4):
        greet(space=2 * lax.rem(z + dz, 4) + xl)

    @pl.when(has_z)
    def _():
        greet(**z_target)

    @pl.when(local)
    def _():
        for i in range(CHUNKS):
            own_chunk(i).start()

    for copy in loads[1:]:
        copy.start()

    column = lax.broadcasted_iota(jnp.int32, (8, 128), 1)
    row8 = lax.broadcasted_iota(jnp.int32, (8, 128), 0)
    meta = jnp.zeros((8, 128), jnp.int32)
    for b in range(2):
        for slot in range(SLOTS):
            meta = jnp.where(column == b * SLOTS + slot, neighbours[b, slot], meta)
    meta = jnp.where(row8 == 2, counts[0], jnp.where(row8 == 3, counts[1], meta))
    meta_v[0] = meta

    @pl.when(jnp.logical_not(has_z))
    def _():
        halo[...] = jnp.zeros_like(halo)

    pl.semaphore_wait(barrier, 34 + has_z.astype(jnp.int32))

    for i in range(CHUNKS // 2):
        x_chunk(2 * i + foreign.astype(jnp.int32)).start()

    @pl.when(local)
    def _():
        meta_copy().start()
        to_scalars = pltpu.make_async_copy(meta_v.at[0], meta_s, lsem.at[10])
        to_scalars.start()
        to_scalars.wait()
        used_v[...] = meta_v[0, 2:4, :]

    def forward(i):
        own_chunk(i).wait()

        @pl.when(has_z)
        def _():
            z_part(0, i, CHUNK).start()

    def normalise(src, row, rows, dst):
        def step(i, _):
            part = pl.ds(pl.multiple_of(row + i * 64, 64), 64)
            values = src[part, :].astype(F32)
            factor = lax.rsqrt(jnp.mean(values * values, axis=-1, keepdims=True) + 1e-06)
            dst[part, :] = (values * factor * gains[...]).astype(BF)
            return 0

        lax.fori_loop(0, rows // 64, step, 0)

    def project(row, rows, w, dst, dst_block):
        values = dot(nrm[pl.ds(row, rows), :], wbuf[w]).astype(BF)
        for i in range(rows // BLOCK):
            dst[w, dst_block + i] = values[i * BLOCK : (i + 1) * BLOCK]

    first_block = 4 * z + 2 * c - 2
    head_of = lax.broadcasted_iota(jnp.int32, (1, TILE), 1)
    masks = [
        jnp.where((head_of >= HEAD * i) & (head_of < HEAD * (i + 1)), 0.125, 0.0).astype(BF) for i in range(4)
    ]
    lane = lax.broadcasted_iota(jnp.int32, (BLOCK, TILE), 1)

    def attend(qkv, b):
        near = [jnp.clip(meta_s[0, b * SLOTS + slot] - first_block, 0, 5) for slot in range(SLOTS)]
        used = used_v[pl.ds(b, 1), :]
        bias = [jnp.where(used > slot, 0.0, -1e30) for slot in range(SLOTS)]

        def scores(g):
            cols = slice(g * TILE, (g + 1) * TILE)
            query = qkv[0, 2 + b, :, cols]
            query = jnp.concatenate([query * mask for mask in masks], axis=0)
            keys = [jnp.concatenate([qkv[1, near[i + k], :, cols] for k in range(2)], axis=0) for i in (0, 2)]
            first = dot_t(query, keys[0])
            second = dot_t(query, keys[1])
            second = jnp.concatenate([second[:, :BLOCK] + bias[2], second[:, BLOCK:] + bias[3]], axis=1)
            return jnp.concatenate([first, second], axis=1)

        ready = scores(0)
        for g in range(D // TILE):
            later = scores(g + 1) if g + 1 < D // TILE else None
            cols = slice(g * TILE, (g + 1) * TILE)
            values = jnp.concatenate([qkv[2, near[i], :, cols] for i in range(SLOTS)], axis=0)
            highest = jnp.max(ready, axis=-1, keepdims=True)
            raised = jnp.exp(ready - highest)
            total = jnp.sum(raised, axis=-1, keepdims=True)
            mixed = dot(raised.astype(BF), values) * (1.0 / total)
            parts = [mixed[i * BLOCK : (i + 1) * BLOCK] for i in range(4)]
            attended = parts[3]
            for i in (2, 1, 0):
                attended = jnp.where(lane < HEAD * (i + 1), parts[i], attended)
            att[:, cols] = attended.astype(BF)
            ready = later

    def update(t, b):
        part = pl.ds(pl.multiple_of(b * BLOCK, BLOCK), BLOCK)
        cur[t + 1, part, :] = (cur[t, part, :].astype(F32) + dot(att[...], wbuf[3])).astype(BF)

    def decode(t, b):
        part = pl.ds(pl.multiple_of(b * BLOCK, BLOCK), BLOCK)
        preds[t, b] = dot(cur[t + 1, part, :], wdec[...]).astype(BF)
        for i in range(8):
            own = local & (c == t) & (m == i)

            @pl.when(own)
            def _():
                preds_own(t, b, i).start()

            @pl.when(jnp.logical_not(own))
            def _():
                preds_copy(t, b, i).start()

    for t in range(STEPS):
        qkv = qkvs[t]
        out_here = local & (c == t)
        if t == 0:
            for i in range(4):
                forward(i)
            loads[5].wait()
            normalise(cur.at[0], 0, BLOCK, nrm)
            forward(4)
            for j, load, chunk in ((1, 0, 5), (2, 1, 6), (0, 2, 7)):
                loads[load].wait()
                project(0, BLOCK, j, qkv, 2)
                if j:
                    kv_copy(0, j, 0).start()
                forward(chunk)
            normalise(cur.at[0], BLOCK, BLOCK, nrm)
            for j in (1, 2, 0):
                project(BLOCK, BLOCK, j, qkv, 3)
                if j:
                    kv_copy(0, j, 1).start()

            @pl.when(foreign)
            def _():
                meta_copy().wait_recv()
                to_scalars = pltpu.make_async_copy(meta_v.at[1], meta_s, lsem.at[10])
                to_scalars.start()
                to_scalars.wait()
                used_v[...] = meta_v[1, 2:4, :]

        else:
            normalise(cur.at[t], 0, ROWS, nrm)
            for j in (1, 2, 0):
                project(0, ROWS, j, qkv, 2)
                if j:
                    for b in range(2):
                        kv_copy(t, j, b).start()
        size = CHUNK if t == 0 else BLOCK
        for b in range(2):

            @pl.when(has_z)
            def _():
                for i in range(BLOCK // size):
                    z_part(t, b * (BLOCK // size) + i, size).wait_recv()

            normalise(halo.at[t], b * BLOCK, BLOCK, nrm)
            for j in (1, 2):
                project(b * BLOCK, BLOCK, j, qkv, 4 * c + b)
            if t == 1 and b == 0:
                loads[4].wait()
                for k in range(2):
                    decode(0, k)
        for j in (1, 2):
            for b in range(2):
                kv_copy(t, j, b).wait_recv()
        if t == 0:
            loads[3].wait()

        def block(b, _):
            attend(qkv, b)
            update(t, b)
            if t + 1 < STEPS:

                @pl.when(has_z)
                def _():
                    z_part(t + 1, b, BLOCK).start()

            if t + 1 == STEPS:
                decode(t, b)

            @pl.when(out_here)
            def _():
                out_local(t, b, xl).start()

            @pl.when(jnp.logical_not(out_here))
            def _():
                out_remote(t, b, xl).start()

            return 0

        lax.fori_loop(0, 2, block, 0)

    for copy in loads[6:10]:
        copy.wait()
    pltpu.make_async_copy(gathered, gathered, pr.at[0]).wait()
    epsilon = (1.0 - ALPHA) / MEMBERS
    weighted = jnp.zeros((1, VARS), F32)
    place = lax.broadcasted_iota(jnp.int32, (SHARE, ROWS), 1) - lax.broadcasted_iota(jnp.int32, (SHARE, ROWS), 0)
    area_sum = jnp.zeros((1, 1), F32)
    for b in range(2):
        weights = jnp.where(place == b * BLOCK + m * SHARE, areas[...], 0.0)
        weights = jnp.sum(weights, axis=1, keepdims=True)
        area_sum += jnp.sum(weights, axis=0, keepdims=True)
        values = [gathered[b, k].astype(F32) for k in range(MEMBERS)]
        wanted = goal[b].astype(F32)
        skill = jnp.zeros((SHARE, VARS), F32)
        spread = jnp.zeros((SHARE, VARS), F32)
        for k in range(MEMBERS):
            skill += jnp.abs(values[k] - wanted)
            for j in range(k):
                spread += jnp.abs(values[k] - values[j])
        terms = skill * (1.0 / MEMBERS) - spread * ((1.0 - epsilon) / (MEMBERS * (MEMBERS - 1)))
        weighted += jnp.sum(terms * weights, axis=0, keepdims=True)
    row = lax.broadcasted_iota(jnp.int32, (8, VARS), 0)
    tile = jnp.where(row == 0, weighted, jnp.where(row == 1, area_sum, 0.0))

    def exchange(tile, buffer, send, recv, me, device):
        count = buffer.shape[0]
        buffer[me] = tile

        def copy(i):
            return pltpu.make_async_remote_copy(
                buffer.at[me], buffer.at[me], send.at[i - 1], recv.at[0],
                device_id=device(lax.rem(me + i, count)), device_id_type=MESH,
            )

        for i in range(1, count):
            copy(i).start()
        rest = buffer.at[pl.ds(0, count - 1)]
        pltpu.make_async_copy(rest, rest, recv.at[0]).wait()
        total = buffer[0]
        for i in range(1, count):
            total += buffer[i]
        return total, copy

    def in_plane(i):
        return {"member": lax.div(i, 2), "space": 2 * z + lax.rem(i, 2)}

    tile, copy1 = exchange(tile, red1, r1s, r1r, 2 * m + xl, in_plane)
    tile, copy2 = exchange(tile, red2, r2s, r2r, z, lambda i: {"space": 2 * i + xl})
    slot = lax.broadcasted_iota(jnp.int32, (1, GROUPS), 1)
    result = jnp.zeros((1, GROUPS), F32)
    for g in range(GROUPS):
        share = jnp.sum(jnp.where(groups[...] == g, tile[0:1], 0.0), axis=1, keepdims=True)
        result = jnp.where(slot == g, share, result)
    loss[...] = result / (tile[1:2, :GROUPS] * (VARS // GROUPS))

    for slot_xl in range(2):
        for b in range(2):
            out_local(0, b, slot_xl).wait()

    for i in range(CHUNKS // 2):
        x_chunk(2 * i + foreign.astype(jnp.int32)).wait_send()

    @pl.when(local)
    def _():
        meta_copy().wait_send()

    @pl.when(has_z)
    def _():
        for i in range(CHUNKS):
            z_part(0, i, CHUNK).wait_send()
        for i in range(2):
            z_part(1, i, BLOCK).wait_send()

    for t in range(STEPS):
        out_here = local & (c == t)
        for j in (1, 2):
            for b in range(2):
                kv_copy(t, j, b).wait_send()

        @pl.when(jnp.logical_not(out_here))
        def _():
            for b in range(2):
                out_remote(t, b, xl).wait_send()

        for i in range(8):

            @pl.when(jnp.logical_not(out_here & (m == i)))
            def _():
                for b in range(2):
                    preds_copy(t, b, i).wait_send()

    for i in range(1, 16):
        copy1(i).wait_send()
    for i in range(1, 4):
        copy2(i).wait_send()


def shards(
    state, norm_gain, w_query, w_key, w_value, w_out, w_decode, neighbours, counts, group_ids, area, truth
):
    anywhere = pl.BlockSpec(memory_space=pl.ANY)
    scalars = pl.BlockSpec(memory_space=pltpu.SMEM)
    dma = pltpu.SemaphoreType.DMA
    return pl.pallas_call(
        kernel,
        out_shape=(
            pltpu.VMEM((1, 2, ROWS, D), BF),
            pltpu.VMEM((1, GROUPS), F32),
        ),
        in_specs=[anywhere] * 7 + [scalars] * 2 + [anywhere] * 3,
        out_specs=(anywhere, pl.BlockSpec(memory_space=pltpu.VMEM)),
        scratch_shapes=[
            pltpu.VMEM((STEPS + 1, ROWS, D), BF),
            pltpu.VMEM((STEPS, ROWS, D), BF),
            pltpu.VMEM((ROWS, D), BF),
            pltpu.VMEM((4, D, D), BF),
            pltpu.VMEM((D, VARS), BF),
            pltpu.VMEM((3, 6, BLOCK, D), BF),
            pltpu.VMEM((3, 6, BLOCK, D), BF),
            pltpu.VMEM((BLOCK, D), BF),
            pltpu.VMEM((STEPS, 2, BLOCK, VARS), BF),
            pltpu.VMEM((2, MEMBERS, SHARE, VARS), BF),
            pltpu.VMEM((2, SHARE, VARS), BF),
            pltpu.VMEM((1, D), F32),
            pltpu.VMEM((1, VARS), jnp.int32),
            pltpu.VMEM((1, ROWS), F32),
            pltpu.VMEM((2, 8, 128), jnp.int32),
            pltpu.VMEM((2, 128), jnp.int32),
            pltpu.SMEM((8, 128), jnp.int32),
            pltpu.VMEM((16, 8, VARS), F32),
            pltpu.VMEM((4, 8, VARS), F32),
            dma((11,)),
            dma((CHUNKS,)),
            dma((CHUNKS,)),
            dma((STEPS, CHUNKS)),
            dma((STEPS, CHUNKS)),
            dma((STEPS, 2, 2)),
            dma((STEPS, 2, 2)),
            dma((STEPS, 2)),
            dma((2, 2)),
            dma((STEPS, 2, 8)),
            dma((1,)),
            dma((1,)),
            dma((1,)),
            dma((15,)),
            dma((1,)),
            dma((3,)),
            dma((1,)),
        ],
        compiler_params=pltpu.CompilerParams(
            collective_id=0, has_side_effects=True, vmem_limit_bytes=60 * 1024 * 1024
        ),
        name="rollout",
    )(
        state, norm_gain.reshape(1, D), w_query, w_key, w_value, w_out, w_decode, neighbours, counts,
        group_ids.reshape(1, VARS), area.reshape(1, ROWS), truth,
    )


def solution(mesh):
    return jax.shard_map(
        shards,
        mesh=mesh,
        in_specs=(
            P("member", "space", None),
            P(),
            P(),
            P(),
            P(),
            P(),
            P(),
            P("space", None),
            P("space"),
            P(),
            P("space"),
            P("step", "space", None),
        ),
        out_specs=(P("step", "member", "space", None), P("step", None)),
        check_vma=False,
    )
```

```python
import functools

import jax
import jax.numpy as jnp
from jax import lax
from jax.experimental import pallas as pl
from jax.experimental.pallas import tpu as pltpu
from jax.sharding import PartitionSpec as P

D = 1024
HEAD = 64
VARS = 128
GROUPS = 8
BLOCK = 128
ROWS = 256
MEMBERS = 16
SLOTS = 4
STEPS = 2
ALPHA = 0.95
CHUNKS = 8
CHUNK = ROWS // CHUNKS
TILE = 256
SHARE = 16
ROUNDS = 5
MESH = pl.DeviceIdType.MESH
BF = jnp.bfloat16
F32 = jnp.float32


def dot(a, b):
    return jnp.dot(a, b, preferred_element_type=F32)


def dot_t(a, b):
    return lax.dot_general(a, b, (((1,), (1,)), ((), ())), preferred_element_type=F32)


def kernel(
    state, gain, w_query, w_key, w_value, w_out, w_decode, neighbours, counts, group_ids, area, truth,
    out, loss,
    cur, halo, nrm, wbuf, wdec, qkv0, qkv1, att, preds, gathered, goal, gains, groups, areas, meta_v, used_v, meta_s,
    red,
    lsem, xs, xr, zs, zr, ks, kr, osend, orecv, ps, pr, ms, mr, rs, rr, rounds,
):
    m, s, c = (lax.axis_index(name) for name in ("member", "space", "step"))
    z, xl = lax.div(s, 2), lax.rem(s, 2)
    local = xl == c
    foreign = xl != c
    partner = {"space": 2 * z + 1 - xl}
    other = {"step": 1 - c}
    has_z = jnp.where(c == 1, z < 3, z > 0)
    z_target = {"space": s + 4 * c - 2, "step": 1 - c}
    qkvs = (qkv0, qkv1)

    def fetch(i, src, dst):
        return pltpu.make_async_copy(src, dst, lsem.at[i])

    loads = [
        fetch(0, w_key, wbuf.at[1]),
        fetch(1, w_value, wbuf.at[2]),
        fetch(2, w_query, wbuf.at[0]),
        fetch(3, w_out, wbuf.at[3]),
        fetch(4, w_decode, wdec),
        fetch(5, gain, gains),
        fetch(6, group_ids, groups),
        fetch(7, area, areas),
        fetch(8, truth.at[0, pl.ds(pl.multiple_of(m * SHARE, SHARE), SHARE)], goal.at[0]),
        fetch(9, truth.at[0, pl.ds(pl.multiple_of(BLOCK + m * SHARE, SHARE), SHARE)], goal.at[1]),
    ]

    def own_chunk(i):
        part = pl.ds(pl.multiple_of(i * CHUNK, CHUNK), CHUNK)
        return pltpu.make_async_copy(state.at[xl, part], cur.at[0, part], xr.at[i])

    def x_chunk(i):
        part = pl.ds(pl.multiple_of(i * CHUNK, CHUNK), CHUNK)
        return pltpu.make_async_remote_copy(
            state.at[1 - xl, part], cur.at[0, part], xs.at[i], xr.at[i],
            device_id={"space": 2 * z + 1 - xl, "step": xl}, device_id_type=MESH,
        )

    def z_part(t, i, size):
        part = pl.ds(pl.multiple_of(i * size, size), size)
        return pltpu.make_async_remote_copy(
            cur.at[t, part], halo.at[t, part], zs.at[t, i], zr.at[t, i], device_id=z_target, device_id_type=MESH
        )

    def meta_copy():
        return pltpu.make_async_remote_copy(
            meta_v.at[0], meta_v.at[1], ms.at[0], mr.at[0], device_id=partner, device_id_type=MESH
        )

    def kv_copy(t, j, b):
        return pltpu.make_async_remote_copy(
            qkvs[t].at[j, 2 + b], qkvs[t].at[j, 4 * c + b], ks.at[t, j - 1, b], kr.at[t, j - 1, b],
            device_id=other, device_id_type=MESH,
        )

    def out_remote(t, b, slot):
        part = pl.ds(pl.multiple_of(b * BLOCK, BLOCK), BLOCK)
        return pltpu.make_async_remote_copy(
            cur.at[t + 1, part], out.at[0, slot, part], osend.at[t, b], orecv.at[slot, b],
            device_id={"space": 2 * z + c, "step": t}, device_id_type=MESH,
        )

    def out_local(t, b, slot):
        part = pl.ds(pl.multiple_of(b * BLOCK, BLOCK), BLOCK)
        return pltpu.make_async_copy(cur.at[t + 1, part], out.at[0, slot, part], orecv.at[slot, b])

    def preds_copy(t, b, i):
        return pltpu.make_async_remote_copy(
            preds.at[t, b, pl.ds(i * SHARE, SHARE)], gathered.at[b, 2 * m + xl], ps.at[t, b, i], pr.at[0],
            device_id={"member": i, "space": 2 * z + c, "step": t}, device_id_type=MESH,
        )

    def preds_own(t, b, i):
        return pltpu.make_async_copy(
            preds.at[t, b, pl.ds(i * SHARE, SHARE)], gathered.at[b, 2 * m + xl], pr.at[0]
        )

    barrier = pltpu.get_barrier_semaphore()

    x = 2 * lax.rem(m, 2) + xl
    y = lax.div(m, 2)
    xs4, ys4, zs4 = ([lax.rem(at + i, 4) for i in range(4)] for at in (x, y, z))

    def chip(dx, dy, dz):
        return {"member": 2 * ys4[dy] + lax.div(xs4[dx], 2), "space": 2 * zs4[dz] + lax.rem(xs4[dx], 2)}

    x_mate = 2 * z + 1 - xl
    across = {"member": 2 * y + 1 - lax.rem(m, 2), "space": x_mate}
    beside = [
        {"space": x_mate},
        {"space": x_mate, "step": 1 - c},
        other,
        across,
        chip(0, 1, 0),
        chip(0, 3, 0),
        chip(0, 0, 1),
        chip(0, 0, 3),
    ]
    near_count = len(beside) + has_z.astype(jnp.int32)

    def greet(semaphore):
        for device in beside:
            pl.semaphore_signal(semaphore, inc=1, device_id=device, device_id_type=MESH)

        @pl.when(has_z)
        def _():
            pl.semaphore_signal(semaphore, inc=1, device_id=z_target, device_id_type=MESH)

    def meet(k):
        if k > 0:
            pl.semaphore_wait(rounds.at[k - 1], near_count)
        if k < ROUNDS:
            greet(rounds.at[k])

    greet(barrier)

    @pl.when(local)
    def _():
        for i in range(CHUNKS):
            own_chunk(i).start()

    for copy in loads:
        copy.start()

    pl.semaphore_wait(barrier, near_count)

    for i in range(CHUNKS // 2):
        x_chunk(2 * i + foreign.astype(jnp.int32)).start()

    column = lax.broadcasted_iota(jnp.int32, (8, 128), 1)
    row8 = lax.broadcasted_iota(jnp.int32, (8, 128), 0)
    meta = jnp.zeros((8, 128), jnp.int32)
    for b in range(2):
        for slot in range(SLOTS):
            meta = jnp.where(column == b * SLOTS + slot, neighbours[b, slot], meta)
    meta = jnp.where(row8 == 2, counts[0], jnp.where(row8 == 3, counts[1], meta))
    meta_v[0] = meta

    @pl.when(jnp.logical_not(has_z))
    def _():
        halo[...] = jnp.zeros_like(halo)

    @pl.when(local)
    def _():
        meta_copy().start()
        to_scalars = pltpu.make_async_copy(meta_v.at[0], meta_s, lsem.at[10])
        to_scalars.start()
        to_scalars.wait()
        used_v[...] = meta_v[0, 2:4, :]

    def forward(i):
        own_chunk(i).wait()

        @pl.when(has_z)
        def _():
            z_part(0, i, CHUNK).start()

    def normalise(src, row, rows, dst):
        def step(i, _):
            part = pl.ds(pl.multiple_of(row + i * 64, 64), 64)
            values = src[part, :].astype(F32)
            factor = lax.rsqrt(jnp.mean(values * values, axis=-1, keepdims=True) + 1e-06)
            dst[part, :] = (values * factor * gains[...]).astype(BF)
            return 0

        lax.fori_loop(0, rows // 64, step, 0)

    def project(row, rows, w, dst, dst_block):
        values = dot(nrm[pl.ds(row, rows), :], wbuf[w]).astype(BF)
        for i in range(rows // BLOCK):
            dst[w, dst_block + i] = values[i * BLOCK : (i + 1) * BLOCK]

    first_block = 4 * z + 2 * c - 2
    head_of = lax.broadcasted_iota(jnp.int32, (1, TILE), 1)
    masks = [
        jnp.where((head_of >= HEAD * i) & (head_of < HEAD * (i + 1)), 0.125, 0.0).astype(BF) for i in range(4)
    ]
    lane = lax.broadcasted_iota(jnp.int32, (BLOCK, TILE), 1)

    def attend(qkv, b):
        near = [jnp.clip(meta_s[0, b * SLOTS + slot] - first_block, 0, 5) for slot in range(SLOTS)]
        used = used_v[pl.ds(b, 1), :]
        bias = [jnp.where(used > slot, 0.0, -1e30) for slot in range(SLOTS)]

        def scores(g):
            cols = slice(g * TILE, (g + 1) * TILE)
            query = qkv[0, 2 + b, :, cols]
            query = jnp.concatenate([query * mask for mask in masks], axis=0)
            keys = [jnp.concatenate([qkv[1, near[i + k], :, cols] for k in range(2)], axis=0) for i in (0, 2)]
            first = dot_t(query, keys[0])
            second = dot_t(query, keys[1])
            second = jnp.concatenate([second[:, :BLOCK] + bias[2], second[:, BLOCK:] + bias[3]], axis=1)
            return jnp.concatenate([first, second], axis=1)

        ready = scores(0)
        for g in range(D // TILE):
            later = scores(g + 1) if g + 1 < D // TILE else None
            cols = slice(g * TILE, (g + 1) * TILE)
            values = jnp.concatenate([qkv[2, near[i], :, cols] for i in range(SLOTS)], axis=0)
            highest = jnp.max(ready, axis=-1, keepdims=True)
            raised = jnp.exp(ready - highest)
            total = jnp.sum(raised, axis=-1, keepdims=True)
            mixed = dot(raised.astype(BF), values) * (1.0 / total)
            parts = [mixed[i * BLOCK : (i + 1) * BLOCK] for i in range(4)]
            attended = parts[3]
            for i in (2, 1, 0):
                attended = jnp.where(lane < HEAD * (i + 1), parts[i], attended)
            att[:, cols] = attended.astype(BF)
            ready = later

    def update(t, b):
        part = pl.ds(pl.multiple_of(b * BLOCK, BLOCK), BLOCK)
        cur[t + 1, part, :] = (cur[t, part, :].astype(F32) + dot(att[...], wbuf[3])).astype(BF)

    def decode(t, b):
        part = pl.ds(pl.multiple_of(b * BLOCK, BLOCK), BLOCK)
        preds[t, b] = dot(cur[t + 1, part, :], wdec[...]).astype(BF)
        for i in range(8):
            own = local & (c == t) & (m == i)

            @pl.when(own)
            def _():
                preds_own(t, b, i).start()

            @pl.when(jnp.logical_not(own))
            def _():
                preds_copy(t, b, i).start()

    for t in range(STEPS):
        qkv = qkvs[t]
        out_here = local & (c == t)
        if t == 0:
            for i in range(4):
                forward(i)
            loads[5].wait()
            normalise(cur.at[0], 0, BLOCK, nrm)
            forward(4)
            for j, load, chunk in ((1, 0, 5), (2, 1, 6), (0, 2, 7)):
                loads[load].wait()
                project(0, BLOCK, j, qkv, 2)
                if j:
                    kv_copy(0, j, 0).start()
                forward(chunk)
            meet(0)
            normalise(cur.at[0], BLOCK, BLOCK, nrm)
            for j in (1, 2, 0):
                project(BLOCK, BLOCK, j, qkv, 3)
                if j:
                    kv_copy(0, j, 1).start()

            @pl.when(foreign)
            def _():
                meta_copy().wait_recv()
                to_scalars = pltpu.make_async_copy(meta_v.at[1], meta_s, lsem.at[10])
                to_scalars.start()
                to_scalars.wait()
                used_v[...] = meta_v[1, 2:4, :]

        else:
            meet(2)
            normalise(cur.at[t], 0, ROWS, nrm)
            for j in (1, 2, 0):
                project(0, ROWS, j, qkv, 2)
                if j:
                    for b in range(2):
                        kv_copy(t, j, b).start()
        size = CHUNK if t == 0 else BLOCK
        for b in range(2):

            @pl.when(has_z)
            def _():
                for i in range(BLOCK // size):
                    z_part(t, b * (BLOCK // size) + i, size).wait_recv()

            normalise(halo.at[t], b * BLOCK, BLOCK, nrm)
            for j in (1, 2):
                project(b * BLOCK, BLOCK, j, qkv, 4 * c + b)
            if t == 1 and b == 0:
                meet(3)
                loads[4].wait()
                for k in range(2):
                    decode(0, k)
        for j in (1, 2):
            for b in range(2):
                kv_copy(t, j, b).wait_recv()
        meet(1 if t == 0 else 4)
        if t == 0:
            loads[3].wait()

        def block(b, _):
            attend(qkv, b)
            update(t, b)
            if t + 1 < STEPS:

                @pl.when(has_z)
                def _():
                    z_part(t + 1, b, BLOCK).start()

            if t + 1 == STEPS:
                decode(t, b)

            @pl.when(out_here)
            def _():
                out_local(t, b, xl).start()

            @pl.when(jnp.logical_not(out_here))
            def _():
                out_remote(t, b, xl).start()

            return 0

        lax.fori_loop(0, 2, block, 0)

    for copy in loads[6:10]:
        copy.wait()
    pltpu.make_async_copy(gathered, gathered, pr.at[0]).wait()
    epsilon = (1.0 - ALPHA) / MEMBERS
    weighted = jnp.zeros((1, VARS), F32)
    place = lax.broadcasted_iota(jnp.int32, (SHARE, ROWS), 1) - lax.broadcasted_iota(jnp.int32, (SHARE, ROWS), 0)
    area_sum = jnp.zeros((1, 1), F32)
    for b in range(2):
        weights = jnp.where(place == b * BLOCK + m * SHARE, areas[...], 0.0)
        weights = jnp.sum(weights, axis=1, keepdims=True)
        area_sum += jnp.sum(weights, axis=0, keepdims=True)
        values = [gathered[b, k].astype(F32) for k in range(MEMBERS)]
        wanted = goal[b].astype(F32)
        skill = jnp.zeros((SHARE, VARS), F32)
        spread = jnp.zeros((SHARE, VARS), F32)
        for k in range(MEMBERS):
            skill += jnp.abs(values[k] - wanted)
            for j in range(k):
                spread += jnp.abs(values[k] - values[j])
        terms = skill * (1.0 / MEMBERS) - spread * ((1.0 - epsilon) / (MEMBERS * (MEMBERS - 1)))
        weighted += jnp.sum(terms * weights, axis=0, keepdims=True)
    slot = lax.broadcasted_iota(jnp.int32, (1, VARS), 1)
    line = jnp.where(slot == GROUPS, area_sum, 0.0)
    for g in range(GROUPS):
        share = jnp.sum(jnp.where(groups[...] == g, weighted, 0.0), axis=1, keepdims=True)
        line = jnp.where(slot == g, share, line)
    meet(ROUNDS)
    place = 8 * m + s
    red[place] = line
    steps = [(dx, dy, dz) for dx in range(4) for dy in range(4) for dz in range(4)]
    steps.sort(key=lambda step: -sum(min(d, 4 - d) for d in step))
    for step in steps[:-1]:
        pltpu.make_async_remote_copy(
            red.at[place], red.at[place], rs.at[0], rr.at[0], device_id=chip(*step), device_id_type=MESH
        ).start()
    rest = red.at[pl.ds(0, 63)]
    pltpu.make_async_copy(rest, rest, rr.at[0]).wait()
    line = jnp.sum(red[...], axis=0)
    loss[...] = line[:, :GROUPS] / (line[:, GROUPS : GROUPS + 1] * (VARS // GROUPS))

    for slot_xl in range(2):
        for b in range(2):
            out_local(0, b, slot_xl).wait()

    for i in range(CHUNKS // 2):
        x_chunk(2 * i + foreign.astype(jnp.int32)).wait_send()

    @pl.when(local)
    def _():
        meta_copy().wait_send()

    @pl.when(has_z)
    def _():
        for i in range(CHUNKS):
            z_part(0, i, CHUNK).wait_send()
        for i in range(2):
            z_part(1, i, BLOCK).wait_send()

    for t in range(STEPS):
        out_here = local & (c == t)
        for j in (1, 2):
            for b in range(2):
                kv_copy(t, j, b).wait_send()

        @pl.when(jnp.logical_not(out_here))
        def _():
            for b in range(2):
                out_remote(t, b, xl).wait_send()

        for i in range(8):

            @pl.when(jnp.logical_not(out_here & (m == i)))
            def _():
                for b in range(2):
                    preds_copy(t, b, i).wait_send()

    pltpu.make_async_copy(rest, rest, rs.at[0]).wait()


def shards(
    state, norm_gain, w_query, w_key, w_value, w_out, w_decode, neighbours, counts, group_ids, area, truth
):
    anywhere = pl.BlockSpec(memory_space=pl.ANY)
    scalars = pl.BlockSpec(memory_space=pltpu.SMEM)
    dma = pltpu.SemaphoreType.DMA
    return pl.pallas_call(
        kernel,
        out_shape=(
            pltpu.VMEM((1, 2, ROWS, D), BF),
            pltpu.VMEM((1, GROUPS), F32),
        ),
        in_specs=[anywhere] * 7 + [scalars] * 2 + [anywhere] * 3,
        out_specs=(anywhere, pl.BlockSpec(memory_space=pltpu.VMEM)),
        scratch_shapes=[
            pltpu.VMEM((STEPS + 1, ROWS, D), BF),
            pltpu.VMEM((STEPS, ROWS, D), BF),
            pltpu.VMEM((ROWS, D), BF),
            pltpu.VMEM((4, D, D), BF),
            pltpu.VMEM((D, VARS), BF),
            pltpu.VMEM((3, 6, BLOCK, D), BF),
            pltpu.VMEM((3, 6, BLOCK, D), BF),
            pltpu.VMEM((BLOCK, D), BF),
            pltpu.VMEM((STEPS, 2, BLOCK, VARS), BF),
            pltpu.VMEM((2, MEMBERS, SHARE, VARS), BF),
            pltpu.VMEM((2, SHARE, VARS), BF),
            pltpu.VMEM((1, D), F32),
            pltpu.VMEM((1, VARS), jnp.int32),
            pltpu.VMEM((1, ROWS), F32),
            pltpu.VMEM((2, 8, 128), jnp.int32),
            pltpu.VMEM((2, 128), jnp.int32),
            pltpu.SMEM((8, 128), jnp.int32),
            pltpu.VMEM((64, 1, VARS), F32),
            dma((11,)),
            dma((CHUNKS,)),
            dma((CHUNKS,)),
            dma((STEPS, CHUNKS)),
            dma((STEPS, CHUNKS)),
            dma((STEPS, 2, 2)),
            dma((STEPS, 2, 2)),
            dma((STEPS, 2)),
            dma((2, 2)),
            dma((STEPS, 2, 8)),
            dma((1,)),
            dma((1,)),
            dma((1,)),
            dma((1,)),
            dma((1,)),
            pltpu.SemaphoreType.REGULAR((ROUNDS,)),
        ],
        compiler_params=pltpu.CompilerParams(
            collective_id=0, has_side_effects=True, vmem_limit_bytes=60 * 1024 * 1024
        ),
        name="rollout",
    )(
        state, norm_gain.reshape(1, D), w_query, w_key, w_value, w_out, w_decode, neighbours, counts,
        group_ids.reshape(1, VARS), area.reshape(1, ROWS), truth,
    )


def solution(mesh):
    return jax.shard_map(
        shards,
        mesh=mesh,
        in_specs=(
            P("member", "space", None),
            P(),
            P(),
            P(),
            P(),
            P(),
            P(),
            P("space", None),
            P("space"),
            P(),
            P("space"),
            P("step", "space", None),
        ),
        out_specs=(P("step", "member", "space", None), P("step", None)),
        check_vma=False,
    )
```

```python
import functools

import jax
import jax.numpy as jnp
from jax import lax
from jax.experimental import pallas as pl
from jax.experimental.pallas import tpu as pltpu
from jax.sharding import PartitionSpec as P

D = 1024
HEAD = 64
VARS = 128
GROUPS = 8
BLOCK = 128
ROWS = 256
MEMBERS = 16
SLOTS = 4
STEPS = 2
ALPHA = 0.95
CHUNKS = 8
CHUNK = ROWS // CHUNKS
TILE = 256
SHARE = 16
ROUNDS = 5
MESH = pl.DeviceIdType.MESH
BF = jnp.bfloat16
F32 = jnp.float32


def dot(a, b):
    return jnp.dot(a, b, preferred_element_type=F32)


def dot_t(a, b):
    return lax.dot_general(a, b, (((1,), (1,)), ((), ())), preferred_element_type=F32)


def kernel(
    state, gain, w_query, w_key, w_value, w_out, w_decode, neighbours, counts, group_ids, area, truth,
    out, loss,
    cur, halo, nrm, wbuf, wdec, qkv0, qkv1, att, preds, gathered, goal, gains, groups, areas, meta_v, used_v, meta_s,
    red,
    lsem, xs, xr, zs, zr, ks, kr, osend, orecv, ps, pr, ms, mr, rs, rr, rounds,
):
    m, s, c = (lax.axis_index(name) for name in ("member", "space", "step"))
    z, xl = lax.div(s, 2), lax.rem(s, 2)
    local = xl == c
    foreign = xl != c
    partner = {"space": 2 * z + 1 - xl}
    other = {"step": 1 - c}
    has_z = jnp.where(c == 1, z < 3, z > 0)
    z_target = {"space": s + 4 * c - 2, "step": 1 - c}
    qkvs = (qkv0, qkv1)

    def fetch(i, src, dst):
        return pltpu.make_async_copy(src, dst, lsem.at[i])

    loads = [
        fetch(0, w_key, wbuf.at[1]),
        fetch(1, w_value, wbuf.at[2]),
        fetch(2, w_query, wbuf.at[0]),
        fetch(3, w_out, wbuf.at[3]),
        fetch(4, w_decode, wdec),
        fetch(5, gain, gains),
        fetch(6, group_ids, groups),
        fetch(7, area, areas),
        fetch(8, truth.at[0, pl.ds(pl.multiple_of(m * SHARE, SHARE), SHARE)], goal.at[0]),
        fetch(9, truth.at[0, pl.ds(pl.multiple_of(BLOCK + m * SHARE, SHARE), SHARE)], goal.at[1]),
    ]

    def own_chunk(i):
        part = pl.ds(pl.multiple_of(i * CHUNK, CHUNK), CHUNK)
        return pltpu.make_async_copy(state.at[xl, part], cur.at[0, part], xr.at[i])

    def x_chunk(i):
        part = pl.ds(pl.multiple_of(i * CHUNK, CHUNK), CHUNK)
        return pltpu.make_async_remote_copy(
            state.at[1 - xl, part], cur.at[0, part], xs.at[i], xr.at[i],
            device_id={"space": 2 * z + 1 - xl, "step": xl}, device_id_type=MESH,
        )

    def z_part(t, i, size):
        part = pl.ds(pl.multiple_of(i * size, size), size)
        return pltpu.make_async_remote_copy(
            cur.at[t, part], halo.at[t, part], zs.at[t, i], zr.at[t, i], device_id=z_target, device_id_type=MESH
        )

    def meta_copy():
        return pltpu.make_async_remote_copy(
            meta_v.at[0], meta_v.at[1], ms.at[0], mr.at[0], device_id=partner, device_id_type=MESH
        )

    def kv_copy(t, j, b):
        return pltpu.make_async_remote_copy(
            qkvs[t].at[j, 2 + b], qkvs[t].at[j, 4 * c + b], ks.at[t, j - 1, b], kr.at[t, j - 1, b],
            device_id=other, device_id_type=MESH,
        )

    def out_remote(t, b, slot):
        part = pl.ds(pl.multiple_of(b * BLOCK, BLOCK), BLOCK)
        return pltpu.make_async_remote_copy(
            cur.at[t + 1, part], out.at[0, slot, part], osend.at[t, b], orecv.at[slot, b],
            device_id={"space": 2 * z + c, "step": t}, device_id_type=MESH,
        )

    def out_local(t, b, slot):
        part = pl.ds(pl.multiple_of(b * BLOCK, BLOCK), BLOCK)
        return pltpu.make_async_copy(cur.at[t + 1, part], out.at[0, slot, part], orecv.at[slot, b])

    def preds_part(t, b, k):
        i = lax.rem(m + k, 8)
        return preds.at[t, b, pl.ds(pl.multiple_of(i * SHARE, SHARE), SHARE)], gathered.at[b, 2 * m + xl], i

    def preds_copy(t, b, k):
        src, dst, i = preds_part(t, b, k)
        return pltpu.make_async_remote_copy(
            src, dst, ps.at[t, b, k], pr.at[b],
            device_id={"member": i, "space": 2 * z + c, "step": t}, device_id_type=MESH,
        )

    def preds_own(t, b):
        src, dst, _ = preds_part(t, b, 0)
        return pltpu.make_async_copy(src, dst, pr.at[b])

    barrier = pltpu.get_barrier_semaphore()

    x = 2 * lax.rem(m, 2) + xl
    y = lax.div(m, 2)
    xs4, ys4, zs4 = ([lax.rem(at + i, 4) for i in range(4)] for at in (x, y, z))

    def chip(dx, dy, dz):
        return {"member": 2 * ys4[dy] + lax.div(xs4[dx], 2), "space": 2 * zs4[dz] + lax.rem(xs4[dx], 2)}

    x_mate = 2 * z + 1 - xl
    across = {"member": 2 * y + 1 - lax.rem(m, 2), "space": x_mate}
    beside = [
        {"space": x_mate},
        {"space": x_mate, "step": 1 - c},
        other,
        across,
        chip(0, 1, 0),
        chip(0, 3, 0),
        chip(0, 0, 1),
        chip(0, 0, 3),
    ]
    near_count = len(beside) + has_z.astype(jnp.int32)

    def greet(semaphore):
        for device in beside:
            pl.semaphore_signal(semaphore, inc=1, device_id=device, device_id_type=MESH)

        @pl.when(has_z)
        def _():
            pl.semaphore_signal(semaphore, inc=1, device_id=z_target, device_id_type=MESH)

    def meet(k):
        if k > 0:
            pl.semaphore_wait(rounds.at[k - 1], near_count)
        if k < ROUNDS:
            greet(rounds.at[k])

    greet(barrier)

    pl.semaphore_wait(barrier, near_count)

    for i in range(CHUNKS // 2):
        x_chunk(2 * i + foreign.astype(jnp.int32)).start()

    @pl.when(local)
    def _():
        for i in range(CHUNKS):
            own_chunk(i).start()

    for copy in loads:
        copy.start()

    column = lax.broadcasted_iota(jnp.int32, (8, 128), 1)
    row8 = lax.broadcasted_iota(jnp.int32, (8, 128), 0)
    meta = jnp.zeros((8, 128), jnp.int32)
    for b in range(2):
        for slot in range(SLOTS):
            meta = jnp.where(column == b * SLOTS + slot, neighbours[b, slot], meta)
    meta = jnp.where(row8 == 2, counts[0], jnp.where(row8 == 3, counts[1], meta))
    meta_v[0] = meta

    @pl.when(jnp.logical_not(has_z))
    def _():
        halo[...] = jnp.zeros_like(halo)

    @pl.when(local)
    def _():
        meta_copy().start()
        to_scalars = pltpu.make_async_copy(meta_v.at[0], meta_s, lsem.at[10])
        to_scalars.start()
        to_scalars.wait()
        used_v[...] = meta_v[0, 2:4, :]

    def forward(i):
        own_chunk(i).wait()

        @pl.when(has_z)
        def _():
            z_part(0, i, CHUNK).start()

    def normalise(src, row, rows, dst):
        def step(i, _):
            part = pl.ds(pl.multiple_of(row + i * 64, 64), 64)
            values = src[part, :].astype(F32)
            factor = lax.rsqrt(jnp.mean(values * values, axis=-1, keepdims=True) + 1e-06)
            dst[part, :] = (values * factor * gains[...]).astype(BF)
            return 0

        lax.fori_loop(0, rows // 64, step, 0)

    def project(row, rows, w, dst, dst_block):
        values = dot(nrm[pl.ds(row, rows), :], wbuf[w]).astype(BF)
        for i in range(rows // BLOCK):
            dst[w, dst_block + i] = values[i * BLOCK : (i + 1) * BLOCK]

    first_block = 4 * z + 2 * c - 2
    head_of = lax.broadcasted_iota(jnp.int32, (1, TILE), 1)
    masks = [
        jnp.where((head_of >= HEAD * i) & (head_of < HEAD * (i + 1)), 0.125, 0.0).astype(BF) for i in range(4)
    ]
    lane = lax.broadcasted_iota(jnp.int32, (BLOCK, TILE), 1)

    def attend(qkv, b):
        near = [jnp.clip(meta_s[0, b * SLOTS + slot] - first_block, 0, 5) for slot in range(SLOTS)]
        used = used_v[pl.ds(b, 1), :]
        bias = [jnp.where(used > slot, 0.0, -1e30) for slot in range(SLOTS)]

        def scores(g):
            cols = slice(g * TILE, (g + 1) * TILE)
            query = qkv[0, 2 + b, :, cols]
            query = jnp.concatenate([query * mask for mask in masks], axis=0)
            keys = [jnp.concatenate([qkv[1, near[i + k], :, cols] for k in range(2)], axis=0) for i in (0, 2)]
            first = dot_t(query, keys[0])
            second = dot_t(query, keys[1])
            second = jnp.concatenate([second[:, :BLOCK] + bias[2], second[:, BLOCK:] + bias[3]], axis=1)
            return jnp.concatenate([first, second], axis=1)

        ready = scores(0)
        for g in range(D // TILE):
            later = scores(g + 1) if g + 1 < D // TILE else None
            cols = slice(g * TILE, (g + 1) * TILE)
            values = jnp.concatenate([qkv[2, near[i], :, cols] for i in range(SLOTS)], axis=0)
            highest = jnp.max(ready, axis=-1, keepdims=True)
            raised = jnp.exp(ready - highest)
            total = jnp.sum(raised, axis=-1, keepdims=True)
            mixed = dot(raised.astype(BF), values) * (1.0 / total)
            parts = [mixed[i * BLOCK : (i + 1) * BLOCK] for i in range(4)]
            attended = parts[3]
            for i in (2, 1, 0):
                attended = jnp.where(lane < HEAD * (i + 1), parts[i], attended)
            att[:, cols] = attended.astype(BF)
            ready = later

    def update(t, b):
        part = pl.ds(pl.multiple_of(b * BLOCK, BLOCK), BLOCK)
        cur[t + 1, part, :] = (cur[t, part, :].astype(F32) + dot(att[...], wbuf[3])).astype(BF)

    def decode(t, b):
        part = pl.ds(pl.multiple_of(b * BLOCK, BLOCK), BLOCK)
        preds[t, b] = dot(cur[t + 1, part, :], wdec[...]).astype(BF)
        for k in (4, 5, 3, 2, 6, 1, 7):
            preds_copy(t, b, k).start()
        own = local & (c == t)

        @pl.when(own)
        def _():
            preds_own(t, b).start()

        @pl.when(jnp.logical_not(own))
        def _():
            preds_copy(t, b, 0).start()

    for t in range(STEPS):
        qkv = qkvs[t]
        out_here = local & (c == t)
        if t == 0:
            for i in range(4):
                forward(i)
            loads[5].wait()
            normalise(cur.at[0], 0, BLOCK, nrm)
            forward(4)
            for j, load, chunk in ((1, 0, 5), (2, 1, 6), (0, 2, 7)):
                loads[load].wait()
                project(0, BLOCK, j, qkv, 2)
                if j:
                    kv_copy(0, j, 0).start()
                forward(chunk)
            meet(0)
            normalise(cur.at[0], BLOCK, BLOCK, nrm)
            for j in (1, 2, 0):
                project(BLOCK, BLOCK, j, qkv, 3)
                if j:
                    kv_copy(0, j, 1).start()

            @pl.when(foreign)
            def _():
                meta_copy().wait_recv()
                to_scalars = pltpu.make_async_copy(meta_v.at[1], meta_s, lsem.at[10])
                to_scalars.start()
                to_scalars.wait()
                used_v[...] = meta_v[1, 2:4, :]

        else:
            meet(2)
            normalise(cur.at[t], 0, ROWS, nrm)
            for j in (1, 2, 0):
                project(0, ROWS, j, qkv, 2)
                if j:
                    for b in range(2):
                        kv_copy(t, j, b).start()
        size = CHUNK if t == 0 else BLOCK
        for b in range(2):

            @pl.when(has_z)
            def _():
                for i in range(BLOCK // size):
                    z_part(t, b * (BLOCK // size) + i, size).wait_recv()

            normalise(halo.at[t], b * BLOCK, BLOCK, nrm)
            for j in (1, 2):
                project(b * BLOCK, BLOCK, j, qkv, 4 * c + b)
            if t == 1 and b == 0:
                meet(3)
                loads[4].wait()
                for k in range(2):
                    decode(0, k)
        for j in (1, 2):
            for b in range(2):
                kv_copy(t, j, b).wait_recv()
        meet(1 if t == 0 else 4)
        if t == 0:
            loads[3].wait()

        def block(b, _):
            attend(qkv, b)
            update(t, b)
            if t + 1 < STEPS:

                @pl.when(has_z)
                def _():
                    z_part(t + 1, b, BLOCK).start()

            if t + 1 == STEPS:
                decode(t, b)

            @pl.when(out_here)
            def _():
                out_local(t, b, xl).start()

            @pl.when(jnp.logical_not(out_here))
            def _():
                out_remote(t, b, xl).start()

            return 0

        lax.fori_loop(0, 2, block, 0)

    for copy in loads[6:10]:
        copy.wait()
    epsilon = (1.0 - ALPHA) / MEMBERS
    weighted = jnp.zeros((1, VARS), F32)
    place = lax.broadcasted_iota(jnp.int32, (SHARE, ROWS), 1) - lax.broadcasted_iota(jnp.int32, (SHARE, ROWS), 0)
    area_sum = jnp.zeros((1, 1), F32)
    for b in range(2):
        weights = jnp.where(place == b * BLOCK + m * SHARE, areas[...], 0.0)
        weights = jnp.sum(weights, axis=1, keepdims=True)
        area_sum += jnp.sum(weights, axis=0, keepdims=True)
        pltpu.make_async_copy(gathered.at[b], gathered.at[b], pr.at[b]).wait()
        values = [gathered[b, k].astype(F32) for k in range(MEMBERS)]
        wanted = goal[b].astype(F32)
        skill = jnp.zeros((SHARE, VARS), F32)
        spread = jnp.zeros((SHARE, VARS), F32)
        for k in range(MEMBERS):
            skill += jnp.abs(values[k] - wanted)
            for j in range(k):
                spread += jnp.abs(values[k] - values[j])
        terms = skill * (1.0 / MEMBERS) - spread * ((1.0 - epsilon) / (MEMBERS * (MEMBERS - 1)))
        weighted += jnp.sum(terms * weights, axis=0, keepdims=True)
    slot = lax.broadcasted_iota(jnp.int32, (1, VARS), 1)
    line = jnp.where(slot == GROUPS, area_sum, 0.0)
    for g in range(GROUPS):
        share = jnp.sum(jnp.where(groups[...] == g, weighted, 0.0), axis=1, keepdims=True)
        line = jnp.where(slot == g, share, line)
    meet(ROUNDS)
    place = 8 * m + s
    red[place] = line
    steps = [(dx, dy, dz) for dx in range(4) for dy in range(4) for dz in range(4)]
    steps.sort(key=lambda step: -sum(min(d, 4 - d) for d in step))
    for step in steps[:-1]:
        pltpu.make_async_remote_copy(
            red.at[place], red.at[place], rs.at[0], rr.at[0], device_id=chip(*step), device_id_type=MESH
        ).start()
    rest = red.at[pl.ds(0, 63)]
    pltpu.make_async_copy(rest, rest, rr.at[0]).wait()
    line = jnp.sum(red[...], axis=0)
    loss[...] = line[:, :GROUPS] / (line[:, GROUPS : GROUPS + 1] * (VARS // GROUPS))

    for slot_xl in range(2):
        for b in range(2):
            out_local(0, b, slot_xl).wait()

    for i in range(CHUNKS // 2):
        x_chunk(2 * i + foreign.astype(jnp.int32)).wait_send()

    @pl.when(local)
    def _():
        meta_copy().wait_send()

    @pl.when(has_z)
    def _():
        for i in range(CHUNKS):
            z_part(0, i, CHUNK).wait_send()
        for i in range(2):
            z_part(1, i, BLOCK).wait_send()

    for t in range(STEPS):
        out_here = local & (c == t)
        for j in (1, 2):
            for b in range(2):
                kv_copy(t, j, b).wait_send()

        @pl.when(jnp.logical_not(out_here))
        def _():
            for b in range(2):
                out_remote(t, b, xl).wait_send()

        for b in range(2):
            for k in range(1, 8):
                preds_copy(t, b, k).wait_send()

            @pl.when(jnp.logical_not(out_here))
            def _():
                preds_copy(t, b, 0).wait_send()

    pltpu.make_async_copy(rest, rest, rs.at[0]).wait()


def shards(
    state, norm_gain, w_query, w_key, w_value, w_out, w_decode, neighbours, counts, group_ids, area, truth
):
    anywhere = pl.BlockSpec(memory_space=pl.ANY)
    scalars = pl.BlockSpec(memory_space=pltpu.SMEM)
    dma = pltpu.SemaphoreType.DMA
    return pl.pallas_call(
        kernel,
        out_shape=(
            pltpu.VMEM((1, 2, ROWS, D), BF),
            pltpu.VMEM((1, GROUPS), F32),
        ),
        in_specs=[anywhere] * 7 + [scalars] * 2 + [anywhere] * 3,
        out_specs=(anywhere, pl.BlockSpec(memory_space=pltpu.VMEM)),
        scratch_shapes=[
            pltpu.VMEM((STEPS + 1, ROWS, D), BF),
            pltpu.VMEM((STEPS, ROWS, D), BF),
            pltpu.VMEM((ROWS, D), BF),
            pltpu.VMEM((4, D, D), BF),
            pltpu.VMEM((D, VARS), BF),
            pltpu.VMEM((3, 6, BLOCK, D), BF),
            pltpu.VMEM((3, 6, BLOCK, D), BF),
            pltpu.VMEM((BLOCK, D), BF),
            pltpu.VMEM((STEPS, 2, BLOCK, VARS), BF),
            pltpu.VMEM((2, MEMBERS, SHARE, VARS), BF),
            pltpu.VMEM((2, SHARE, VARS), BF),
            pltpu.VMEM((1, D), F32),
            pltpu.VMEM((1, VARS), jnp.int32),
            pltpu.VMEM((1, ROWS), F32),
            pltpu.VMEM((2, 8, 128), jnp.int32),
            pltpu.VMEM((2, 128), jnp.int32),
            pltpu.SMEM((8, 128), jnp.int32),
            pltpu.VMEM((64, 1, VARS), F32),
            dma((11,)),
            dma((CHUNKS,)),
            dma((CHUNKS,)),
            dma((STEPS, CHUNKS)),
            dma((STEPS, CHUNKS)),
            dma((STEPS, 2, 2)),
            dma((STEPS, 2, 2)),
            dma((STEPS, 2)),
            dma((2, 2)),
            dma((STEPS, 2, 8)),
            dma((2,)),
            dma((1,)),
            dma((1,)),
            dma((1,)),
            dma((1,)),
            pltpu.SemaphoreType.REGULAR((ROUNDS,)),
        ],
        compiler_params=pltpu.CompilerParams(
            collective_id=0, has_side_effects=True, vmem_limit_bytes=60 * 1024 * 1024
        ),
        name="rollout",
    )(
        state, norm_gain.reshape(1, D), w_query, w_key, w_value, w_out, w_decode, neighbours, counts,
        group_ids.reshape(1, VARS), area.reshape(1, ROWS), truth,
    )


def solution(mesh):
    return jax.shard_map(
        shards,
        mesh=mesh,
        in_specs=(
            P("member", "space", None),
            P(),
            P(),
            P(),
            P(),
            P(),
            P(),
            P("space", None),
            P("space"),
            P(),
            P("space"),
            P("step", "space", None),
        ),
        out_specs=(P("step", "member", "space", None), P("step", None)),
        check_vma=False,
    )
```
